128 devices in a mesh: section: 4 (over x), tensor: 32 (over z, y, core).
Axes of the slice: x: 4, y: 4, z: 4, core: 2. Of those that a mesh axis runs over, the one named last changes fastest.
Arguments:
- inputs: bfloat16 [4, 128, 4096], P(None, None, 'tensor'), may hold values from -6 to 6
- grad_out: bfloat16 [4, 128, 4096], P(None, None, 'tensor'), may hold values from -6 to 6
- tenants: int32 [4], replicated, may hold values from 0 to 3, each once
- base_weight: bfloat16 [4, 4096, 4096], P('section', None, 'tensor'), may hold values from -0.09375 to 0.09375
- adapter_a: bfloat16 [4, 4, 16, 4096], P('section'), may hold values from -0.09375 to 0.09375
- adapter_b: bfloat16 [4, 4, 16, 4096], P('section', None, None, 'tensor'), may hold values from -1.5 to 1.5
- magnitude: float32 [4, 4, 4096], P('section', None, 'tensor'), may hold values from 0.5 to 1.5
Outputs:
- grad_a: float32 [4, 4, 16, 4096], P('section', None, None, 'tensor')
- grad_b: float32 [4, 4, 16, 4096], P('section', None, None, 'tensor')
- grad_magnitude: float32 [4, 4, 4096], P('section', None, 'tensor')
The draws below stay inside these ranges and needn't reach their ends.
Inputs may be any that keep to these rules, and one draw needn't show every extreme that they name: `tenants`: every tenant serves exactly one micro-batch.
All inputs are finite; a program needn't handle non-finite values.
Results may differ from the reference program's by a relative error of at most 0.008.
Values may be sent and summed in bfloat16 or wider, within the bound.
A program may use at most 64 MiB of HBM per device.

```python
import math
import jax
import jax.numpy as jnp
from jax import lax

D = 4096
RANK = 16
TENANTS = 4
TOK = 128
MICRO = 4
LAYERS = 4


def draw_adapter_a(key, part):
    key = jax.random.fold_in(key, 11)
    key_own, key_common = jax.random.split(key)
    own = jnp.clip(jax.random.normal(key_own, (LAYERS, TENANTS, RANK, D), jnp.float32), -4.0, 4.0)
    common = jnp.clip(jax.random.normal(key_common, (LAYERS, TENANTS, 1, D), jnp.float32), -4.0, 4.0)
    share = 0.5
    mixed = math.sqrt(1.0 - share) * own + math.sqrt(share) * common
    return (mixed * D ** (-0.5)).astype(jnp.bfloat16)


def block_scale(key, dims, cuts, least, high):
    def one(position, parts):
        draws = jax.random.uniform(jax.random.fold_in(jax.random.fold_in(key, 6), position), (parts,), jnp.float32, least / len(cuts), high / len(cuts))
        return jnp.repeat(jnp.exp(draws), dims[position] // parts).reshape((-1,) + (1,) * (len(dims) - position - 1))

    gain = one(*cuts[0])
    for cut in cuts[1:]:
        gain = gain * one(*cut)
    return gain


def centred(rng, shape, deviation, bound, shards=(), held_as=jnp.bfloat16):
    factor_of = block_scale(rng, shape, shards, -0.22, 0.18) if shards else 1.0
    drawn = jax.random.normal(rng, shape, jnp.float32) * deviation * factor_of
    return jnp.minimum(jnp.maximum(drawn, -bound), bound).astype(held_as)


def setup_inputs(seed: int = 0) -> dict:
    key_of = jax.random.split(jax.random.key(seed), 8)
    return {
        "inputs": centred(key_of[0], (MICRO, TOK, D), 1.0, 6.0, ((2, 32),)),
        "grad_out": centred(key_of[1], (MICRO, TOK, D), 1.0, 6.0, ((2, 32),)),
        "tenants": jax.random.permutation(key_of[2], TENANTS).astype(jnp.int32),
        "base_weight": centred(key_of[3], (LAYERS, D, D), D ** -0.5, 0.09375, ((0, 4), (2, 32))),
        "adapter_a": draw_adapter_a(jax.random.fold_in(key_of[7], 71), 0),
        "adapter_b": centred(key_of[5], (LAYERS, TENANTS, RANK, D), RANK ** -0.5, 1.5, ((0, 4), (3, 32))),
        "magnitude": jnp.clip(1.0 + 0.1 * jax.random.normal(key_of[6], (LAYERS, TENANTS, D), jnp.float32), 0.5, 1.5),
    }


def column_norms(w_base, a_all, b_all):
    wide = w_base.astype(jnp.float32)
    base_sq = lax.optimization_barrier(jnp.sum(wide * wide, axis=0))
    a_wide = a_all.astype(jnp.float32)
    b_wide = b_all.astype(jnp.float32)
    cross = jnp.einsum('trd,dc->trc', a_wide, wide, precision=lax.Precision.HIGHEST)
    gram = jnp.einsum('trd,tsd->trs', a_wide, a_wide, precision=lax.Precision.HIGHEST)
    quad = jnp.einsum('trs,tsc->trc', gram, b_wide, precision=lax.Precision.HIGHEST)
    total = base_sq[None, :] + lax.optimization_barrier(jnp.sum(b_wide * (2.0 * cross + quad), axis=1))
    return jnp.sqrt(total + 1e-06)

def reference(inputs, grad_out, tenants, base_weight, adapter_a, adapter_b, magnitude):
    layers, tenant_count, rank, width = adapter_a.shape
    micro, tokens_mb = (inputs.shape[0], inputs.shape[1])
    highest = lax.Precision.HIGHEST
    saved = []
    state = inputs
    for layer in range(layers):
        norms = column_norms(base_weight[layer], adapter_a[layer], adapter_b[layer])
        a_sel = adapter_a[layer][tenants].astype(jnp.float32)
        b_sel = adapter_b[layer][tenants].astype(jnp.float32)
        norm_sel = norms[tenants]
        scale = magnitude[layer][tenants] / norm_sel
        wide = state.astype(jnp.float32)
        root = jnp.sqrt(lax.optimization_barrier(jnp.mean(wide * wide, axis=-1, keepdims=True)) + 1e-05)
        normed = (wide / root).astype(jnp.bfloat16)
        lowrank = jnp.einsum('mtd,mrd->mtr', normed.astype(jnp.float32), a_sel, precision=highest).astype(jnp.bfloat16)
        base = jnp.dot(normed.reshape(-1, width), base_weight[layer], preferred_element_type=jnp.float32)
        branch = base.reshape(micro, tokens_mb, width) + jnp.einsum('mtr,mrc->mtc', lowrank.astype(jnp.float32), b_sel, precision=highest)
        saved.append((state, root, normed, lowrank, branch, norm_sel, scale, a_sel, b_sel))
        state = (wide + scale[:, None, :] * branch).astype(jnp.bfloat16)
    grad = grad_out
    grads_a, grads_b, grads_m = ([], [], [])
    for layer in reversed(range(layers)):
        state, root, normed, lowrank, branch, norm_sel, scale, a_sel, b_sel = saved[layer]
        wide = state.astype(jnp.float32)
        upstream = grad.astype(jnp.float32)
        grad_mag = lax.optimization_barrier(jnp.sum(upstream * branch, axis=1)) / norm_sel
        grad_branch = (upstream * scale[:, None, :]).astype(jnp.bfloat16)
        branch_wide = grad_branch.astype(jnp.float32)
        grad_b = jnp.einsum('mtr,mtc->mrc', lowrank.astype(jnp.float32), branch_wide, precision=highest)
        rank_sum = jnp.einsum('mtc,mrc->mtr', branch_wide, b_sel, precision=highest)
        grad_h = jnp.dot(grad_branch.reshape(-1, width), base_weight[layer].T, preferred_element_type=jnp.float32)
        grad_h = grad_h.reshape(micro, tokens_mb, width) + jnp.einsum('mtr,mrd->mtd', rank_sum, a_sel, precision=highest)
        grad_a = jnp.einsum('mtr,mtd->mrd', rank_sum, normed.astype(jnp.float32), precision=highest)
        row_dot = lax.optimization_barrier(jnp.sum(grad_h * wide, axis=-1, keepdims=True))
        grad = (upstream + (grad_h - wide * row_dot / (width * root * root)) / root).astype(jnp.bfloat16)
        grads_a.append(jnp.zeros((tenant_count, rank, width), jnp.float32).at[tenants].set(grad_a))
        grads_b.append(jnp.zeros((tenant_count, rank, width), jnp.float32).at[tenants].set(grad_b))
        grads_m.append(jnp.zeros((tenant_count, width), jnp.float32).at[tenants].set(grad_mag))
    total_a = jnp.stack(grads_a[::-1])
    total_b = jnp.stack(grads_b[::-1])
    total_m = jnp.stack(grads_m[::-1])
    mean_a = lax.optimization_barrier(jnp.mean(total_a * total_a, axis=(0, 2, 3)))
    mean_b = lax.optimization_barrier(jnp.mean(total_b * total_b, axis=(0, 2, 3)))
    mean_m = lax.optimization_barrier(jnp.mean(total_m * total_m, axis=(0, 2)))
    out_a = total_a / jnp.sqrt(mean_a + 1e-06)[None, :, None, None]
    out_b = total_b / jnp.sqrt(mean_b + 1e-06)[None, :, None, None]
    out_m = total_m / jnp.sqrt(mean_m + 1e-06)[None, :, None]
    return (out_a, out_b, out_m)
```

```python
import jax
import jax.numpy as jnp
from jax import lax
from jax.experimental import pallas as pl
from jax.experimental.pallas import tpu as pltpu
from jax.sharding import PartitionSpec as P

MESH = pl.DeviceIdType.MESH
F32 = jnp.float32
BF16 = jnp.bfloat16

L = 4
TOK = 128
D = 4096
R = 16
COLS = 128
CHIPS = 16
BLK = TOK + R
EXT = 32
RSB = TOK + EXT
HALF = D // 2
WCH = 8
WROWS = HALF // WCH

OFFSETS = [(dz, dy) for dz in range(4) for dy in range(4)]


def hops(r):
    dz, dy = OFFSETS[r]
    return min(dz, 4 - dz) + min(dy, 4 - dy)


NEAR = sorted(range(1, CHIPS), key=hops)
FAR = NEAR[::-1]


def inverse(r):
    dz, dy = OFFSETS[r]
    return ((4 - dz) % 4) * 4 + (4 - dy) % 4


def dot(a, b, ca, cb, precision=None):
    return lax.dot_general(
        a, b, (((ca,), (cb,)), ((), ())), precision=precision, preferred_element_type=F32
    )


def split3(v):
    hi = v.astype(BF16)
    rest = v - hi.astype(F32)
    mid = rest.astype(BF16)
    low = (rest - mid.astype(F32)).astype(BF16)
    return jnp.concatenate([hi, mid, low], axis=0)


def fold3(v):
    return v[0:R] + v[R : 2 * R] + v[2 * R : 3 * R]


def kernel(
    ten_ref, x_ref, g_ref, w_hbm, a_hbm, b_ref, m_ref,
    oa_ref, ob_ref, om_ref,
    w_buf, a_own, sm_src, mg_src, sm_buf, mg_buf, xg, cur,
    sv_branch, sv_low, sv_root, sv_norm, sv_scale,
    cs_src, cs_dst, ce_src, ce_dst, rs_src, rs_dst, ex_src, ex_dst,
    res, od_src, od_dst,
    loc_sem, w_send, w_recv, sm_send, sm_recv, mg_send, mg_recv,
    ag_send, ag_recv, cf_send, cf_recv,
    cs_send, cs_recv, ce_send, ce_recv, rs_send, rs_recv, ex_send, ex_recv,
    od_send, od_recv,
):
    s = lax.axis_index("section")
    t = lax.axis_index("tensor")
    z = t // 8
    y = (t // 2) % 4
    c = t % 2

    def plane(r):
        dz, dy = OFFSETS[r]
        return (s, ((z + dz) % 4) * 8 + ((y + dy) % 4) * 2 + c)

    def source(r):
        dz, dy = OFFSETS[r]
        return ((z + 4 - dz) % 4) * 4 + (y + 4 - dy) % 4

    partner = (s, t + 1 - 2 * c)

    def section(d):
        return ((s + d) % 4, t)

    def remote(src, dst, send, recv, device):
        return pltpu.make_async_remote_copy(
            src_ref=src, dst_ref=dst, send_sem=send, recv_sem=recv,
            device_id=device, device_id_type=MESH,
        )

    def w_copy(layer, way, j, device, from_hbm=False):
        rows = pl.ds(way * HALF + j * WROWS, WROWS)
        src = w_hbm.at[0, rows] if from_hbm else w_buf.at[layer, rows]
        return remote(
            src, w_buf.at[layer, rows], w_send.at[layer, way, j], w_recv.at[layer, way, j], device
        )

    def sm_copy(d):
        return remote(sm_src.at[d], sm_buf.at[s], sm_send.at[d], sm_recv.at[d], section(d))

    def mg_copy(d):
        return remote(mg_src.at[d], mg_buf.at[s], mg_send.at[d], mg_recv.at[d], section(d))

    def ag_copy(l, r):
        return remote(xg.at[l, 0, c], xg.at[l, r, c], ag_send.at[l, r], ag_recv.at[l, r], plane(r))

    def cf_copy(l, r, core):
        return remote(
            xg.at[l, r, core], xg.at[l, r, core], cf_send.at[l, r], cf_recv.at[l, r], partner
        )

    def cs_copy(l, r):
        return remote(
            cs_src.at[l, r], cs_dst.at[l, r], cs_send.at[l, r], cs_recv.at[l, r], partner
        )

    def ce_copy(l):
        return remote(ce_src.at[l], ce_dst.at[l], ce_send.at[l], ce_recv.at[l], partner)

    def rs_copy(l, r):
        return remote(
            rs_src.at[l, r], rs_dst.at[l, r], rs_send.at[l, r], rs_recv.at[l, r], plane(r)
        )

    def ex_copy(r):
        return remote(ex_src, ex_dst.at[r], ex_send.at[r], ex_recv.at[r], plane(r))

    def od_copy(d):
        return remote(
            od_src.at[(s + d) % 4], od_dst.at[s], od_send.at[d], od_recv.at[d], section(d)
        )

    own_w = pltpu.make_async_copy(w_hbm.at[0], w_buf.at[s], loc_sem.at[0])
    own_w.start()
    own_a = pltpu.make_async_copy(
        a_hbm.at[0, :, :, pl.ds(pl.multiple_of(t * COLS, COLS), COLS)], a_own, loc_sem.at[1]
    )
    own_a.start()
    for j in range(WCH):
        w_copy(s, 0, j, section(1), True).start()
        w_copy(s, 1, j, section(3), True).start()
    own_a.wait()
    for d in range(4):
        tenant = ten_ref[(s + d) % 4]
        pair = jnp.concatenate([a_own[tenant], b_ref[0, tenant]], axis=0)
        mag = jnp.broadcast_to(m_ref[0, pl.ds(tenant, 1), :], (8, COLS))
        if d == 0:
            sm_buf[s] = pair
            mg_buf[s] = mag
        else:
            sm_src[d] = pair
            mg_src[d] = mag
            sm_copy(d).start()
            mg_copy(d).start()
    cur[...] = x_ref[s]
    for d in range(1, 4):
        sm_copy(d).wait_recv()
        mg_copy(d).wait_recv()

    def send_block(l):
        xg[l, 0, c] = jnp.concatenate([cur[...], sm_buf[l, 0:R]], axis=0)
        for r in FAR:
            ag_copy(l, r).start()
        cf_copy(l, 0, c).start()

    send_block(0)

    def hop(h):
        def body(j, _):
            a_layer, b_layer = (s + 4 - h) % 4, (s + h) % 4
            w_copy(a_layer, 0, j, section(1)).wait_recv()
            if h < 3:
                w_copy(a_layer, 0, j, section(1)).start()
            w_copy(b_layer, 1, j, section(3)).wait_recv()
            if h < 3:
                w_copy(b_layer, 1, j, section(3)).start()
            return 0

        lax.fori_loop(0, WCH, body, 0)

    for h in (1, 2, 3):
        hop(h)
    own_w.wait()

    def forward(l, _):
        @pl.when(l > 0)
        def _():
            send_block(l)

        def squares(i, total):
            rows = w_buf[l, pl.ds(pl.multiple_of(i * 256, 256), 256), :].astype(F32)
            return total + jnp.sum((rows * rows).reshape(32, 8, COLS), axis=0)

        base_sq = jnp.sum(
            lax.fori_loop(0, 16, squares, jnp.zeros((8, COLS), F32)), axis=0, keepdims=True
        )

        acc = jnp.zeros((BLK, COLS), F32)
        low_acc = jnp.zeros((BLK, R), F32)
        ssq = jnp.zeros((TOK, COLS), F32)

        def use(r, acc, low_acc, ssq):
            cf_copy(l, r, 1 - c).wait_recv()
            both = jnp.concatenate([xg[l, r, 0], xg[l, r, 1]], axis=1)
            rows = w_buf[l, pl.ds(pl.multiple_of(source(r) * 256, 256), 256), :]
            acc = acc + dot(both, rows, 1, 0)
            low_acc = low_acc + dot(both, both[TOK:BLK], 1, 1)
            wide = both[0:TOK].astype(F32)
            wide = wide * wide
            return acc, low_acc, ssq + wide[:, 0:COLS] + wide[:, COLS:]

        before = 0
        for r in NEAR:
            ag_copy(l, r).wait_recv()
            cf_copy(l, r, c).start()
            acc, low_acc, ssq = use(before, acc, low_acc, ssq)
            before = r
        acc, low_acc, ssq = use(before, acc, low_acc, ssq)

        mean = jnp.sum(ssq, axis=1, keepdims=True) * (1.0 / D)
        root = jnp.sqrt(mean + 1e-05)
        inv = 1.0 / root
        b_l = sm_buf[l, R : 2 * R]
        b_wide = b_l.astype(F32)
        low = (low_acc[0:TOK] * inv).astype(BF16)
        branch = acc[0:TOK] * inv + dot(low, b_l, 1, 0)
        quad = dot(low_acc[TOK:BLK], b_wide, 1, 0, lax.Precision.HIGHEST)
        cross = acc[TOK:BLK]
        total = base_sq + jnp.sum(b_wide * (2.0 * cross + quad), axis=0, keepdims=True)
        norm = jnp.sqrt(total + 1e-06)
        scale = mg_buf[l, 0:1] / norm
        sv_branch[l] = branch
        sv_low[l] = low
        sv_root[l] = jnp.broadcast_to(root, (TOK, COLS))
        sv_norm[l] = jnp.broadcast_to(norm, (8, COLS))
        sv_scale[l] = jnp.broadcast_to(scale, (8, COLS))
        cur[...] = (cur[...].astype(F32) + scale * branch).astype(BF16)
        return 0

    lax.fori_loop(0, L, forward, 0)

    cur[...] = g_ref[s]

    def local_grads(l):
        up = cur[...].astype(F32)
        branch = sv_branch[l]
        grad_branch = (up * sv_scale[l, 0:1]).astype(BF16)
        gm = jnp.sum(up * branch, axis=0, keepdims=True) / sv_norm[l, 0:1]
        gb = dot(sv_low[l], grad_branch, 0, 0)
        rank_t = dot(sm_buf[l, R : 2 * R], grad_branch, 1, 1)
        res[l, R : 2 * R] = gb
        res[l, 2 * R : 2 * R + 8] = jnp.broadcast_to(gm, (8, COLS))
        return up, branch, grad_branch, rank_t

    def adapter_grad(l, rank_sum):
        normed = (xg[l, 0, c, 0:TOK].astype(F32) / sv_root[l]).astype(BF16)
        ga = fold3(dot(split3(rank_sum), normed, 1, 0))
        res[l, 0:R] = ga
        return ga

    def backward(i, _):
        l = L - 1 - i
        up, branch, grad_branch, rank_t = local_grads(l)
        root = sv_root[l]
        prod = grad_branch.astype(F32) * branch * root
        row = jnp.sum(prod.T, axis=0, keepdims=True)
        ce_src[l] = jnp.concatenate([rank_t, jnp.broadcast_to(row, (8, TOK))], axis=0)
        ce_copy(l).start()
        rank = rank_t.T
        rank_hi = rank.astype(BF16)
        rank_lo = (rank - rank_hi.astype(F32)).astype(BF16)
        rank_two = jnp.concatenate([rank_hi, rank_lo], axis=1)

        def part(r, core):
            dest = source(inverse(r))
            start = pl.multiple_of(dest * 256 + core * COLS, COLS)
            rows = w_buf[l, pl.ds(start, COLS), :]
            a_d = xg[l, inverse(r), core, TOK:BLK]
            return dot(grad_branch, rows, 1, 1) + dot(
                rank_two, jnp.concatenate([a_d, a_d], axis=0), 1, 0
            )

        order = FAR + [0]
        for r in order:
            cs_src[l, r] = part(r, 1 - c).astype(BF16)
            cs_copy(l, r).start()
        ce_copy(l).wait_recv()
        ext = ce_src[l] + ce_dst[l]
        row = ext[R : R + 8]
        row_hi = row.astype(BF16).astype(F32)
        ext = jnp.concatenate([ext[0:R], row_hi, row - row_hi], axis=0)
        ext_b = ext.astype(BF16)
        own = None
        for r in order:
            mine = part(r, c)
            cs_copy(l, r).wait_recv()
            mine = mine + cs_dst[l, r].astype(F32)
            if r:
                rs_src[l, r, 0:TOK] = mine.astype(BF16)
                rs_src[l, r, TOK:RSB] = ext_b
                rs_copy(l, r).start()
            else:
                own = mine
        total = jnp.concatenate([own, ext], axis=0)
        for r in NEAR:
            rs_copy(l, r).wait_recv()
            total = total + rs_dst[l, r].astype(F32)
        grad_h = total[0:TOK]
        rank_sum = total[TOK : TOK + R]
        row = total[TOK + R : TOK + R + 1] + total[TOK + R + 8 : TOK + R + 9]
        row_dot = jnp.broadcast_to(row, (TOK, TOK)).T
        x_own = xg[l, 0, c, 0:TOK].astype(F32)
        inv = 1.0 / root
        cur[...] = (up + (grad_h - x_own * (row_dot * (inv * inv) * (1.0 / D))) * inv).astype(BF16)
        adapter_grad(l, rank_sum)
        return 0

    lax.fori_loop(0, L - 1, backward, 0)

    _, _, _, rank_t = local_grads(0)
    sum_a = jnp.zeros((1, COLS), F32)
    sum_b = jnp.zeros((1, COLS), F32)
    sum_m = jnp.zeros((1, COLS), F32)
    for l in range(L):
        if l:
            ga = res[l, 0:R]
            sum_a = sum_a + jnp.sum(ga * ga, axis=0, keepdims=True)
        gb = res[l, R : 2 * R]
        sum_b = sum_b + jnp.sum(gb * gb, axis=0, keepdims=True)
        gm = res[l, 2 * R : 2 * R + 1]
        sum_m = sum_m + gm * gm
    ce_src[0] = jnp.concatenate(
        [rank_t, sum_a, sum_b, sum_m, jnp.zeros((5, COLS), F32)], axis=0
    )
    ce_copy(0).start()
    ce_copy(0).wait_recv()
    ext = ce_src[0] + ce_dst[0]
    ex_src[...] = ext
    for r in FAR:
        ex_copy(r).start()
    for r in NEAR:
        ex_copy(r).wait_recv()
        ext = ext + ex_dst[r]
    rank_sum = ext[0:R]
    adapter_grad(0, rank_sum)
    inv_row = (1.0 / sv_root[0]).T[0:1]
    rank_parts = split3(rank_sum * inv_row)
    sq = jnp.zeros((R, COLS), F32)
    for r in range(CHIPS):
        for core in range(2):
            ga = fold3(dot(rank_parts, xg[0, r, core, 0:TOK], 1, 0))
            sq = sq + ga * ga

    def norm_of(v, count):
        return 1.0 / jnp.sqrt(jnp.sum(v, axis=1, keepdims=True) * (1.0 / count) + 1e-06)

    by_a = norm_of(ext[R : R + 1] + jnp.sum(sq, axis=0, keepdims=True), L * R * D)
    by_b = norm_of(ext[R + 1 : R + 2], L * R * D)
    by_m = norm_of(ext[R + 2 : R + 3], L * D)
    for l in range(L):
        od_src[l, 0:R] = res[l, 0:R] * by_a
        od_src[l, R : 2 * R] = res[l, R : 2 * R] * by_b
        od_src[l, 2 * R : 2 * R + 8] = res[l, 2 * R : 2 * R + 8] * by_m
    for d in (2, 1, 3):
        od_copy(d).start()
    od_dst[s] = od_src[s]
    for d in (1, 3, 2):
        od_copy(d).wait_recv()
    for tenant in range(4):
        out = jnp.zeros((2 * R + 8, COLS), F32)
        for k in range(4):
            out = jnp.where(ten_ref[k] == tenant, od_dst[k], out)
        oa_ref[0, tenant] = out[0:R]
        ob_ref[0, tenant] = out[R : 2 * R]
        om_ref[0, pl.ds(tenant, 1), :] = out[2 * R : 2 * R + 1]

    def drain_w(j, _):
        for h in range(3):
            w_copy((s + 4 - h) % 4, 0, j, section(1)).wait_send()
            w_copy((s + h) % 4, 1, j, section(3)).wait_send()
        return 0

    lax.fori_loop(0, WCH, drain_w, 0)

    def drain_l(l, _):
        for r in range(CHIPS):
            cf_copy(l, r, c).wait_send()
            if r:
                ag_copy(l, r).wait_send()
        ce_copy(l).wait_send()
        return 0

    lax.fori_loop(0, L, drain_l, 0)

    def drain_b(l, _):
        for r in range(CHIPS):
            cs_copy(l, r).wait_send()
            if r:
                rs_copy(l, r).wait_send()
        return 0

    lax.fori_loop(1, L, drain_b, 0)
    for r in range(1, CHIPS):
        ex_copy(r).wait_send()
    for d in range(1, 4):
        sm_copy(d).wait_send()
        mg_copy(d).wait_send()
        od_copy(d).wait_send()


def local(inputs, grad_out, tenants, base_weight, adapter_a, adapter_b, magnitude):
    vmem = pl.BlockSpec(memory_space=pltpu.VMEM)
    hbm = pl.BlockSpec(memory_space=pl.ANY)
    dma = pltpu.SemaphoreType.DMA
    return pl.pallas_call(
        kernel,
        out_shape=(
            jax.ShapeDtypeStruct((1, 4, R, COLS), F32),
            jax.ShapeDtypeStruct((1, 4, R, COLS), F32),
            jax.ShapeDtypeStruct((1, 4, COLS), F32),
        ),
        in_specs=[pl.BlockSpec(memory_space=pltpu.SMEM), vmem, vmem, hbm, hbm, vmem, vmem],
        out_specs=(vmem, vmem, vmem),
        scratch_shapes=[
            pltpu.VMEM((L, D, COLS), BF16),
            pltpu.VMEM((4, R, COLS), BF16),
            pltpu.VMEM((4, 2 * R, COLS), BF16),
            pltpu.VMEM((4, 8, COLS), F32),
            pltpu.VMEM((4, 2 * R, COLS), BF16),
            pltpu.VMEM((4, 8, COLS), F32),
            pltpu.VMEM((L, CHIPS, 2, BLK, COLS), BF16),
            pltpu.VMEM((TOK, COLS), BF16),
            pltpu.VMEM((L, TOK, COLS), F32),
            pltpu.VMEM((L, TOK, R), BF16),
            pltpu.VMEM((L, TOK, COLS), F32),
            pltpu.VMEM((L, 8, COLS), F32),
            pltpu.VMEM((L, 8, COLS), F32),
            pltpu.VMEM((L, CHIPS, TOK, COLS), BF16),
            pltpu.VMEM((L, CHIPS, TOK, COLS), BF16),
            pltpu.VMEM((L, R + 8, TOK), F32),
            pltpu.VMEM((L, R + 8, TOK), F32),
            pltpu.VMEM((L, CHIPS, RSB, COLS), BF16),
            pltpu.VMEM((L, CHIPS, RSB, COLS), BF16),
            pltpu.VMEM((R + 8, TOK), F32),
            pltpu.VMEM((CHIPS, R + 8, TOK), F32),
            pltpu.VMEM((L, 2 * R + 8, COLS), F32),
            pltpu.VMEM((L, 2 * R + 8, COLS), F32),
            pltpu.VMEM((L, 2 * R + 8, COLS), F32),
            dma((2,)),
            dma((L, 2, WCH)),
            dma((L, 2, WCH)),
            dma((4,)),
            dma((4,)),
            dma((4,)),
            dma((4,)),
            dma((L, CHIPS)),
            dma((L, CHIPS)),
            dma((L, CHIPS)),
            dma((L, CHIPS)),
            dma((L, CHIPS)),
            dma((L, CHIPS)),
            dma((L,)),
            dma((L,)),
            dma((L, CHIPS)),
            dma((L, CHIPS)),
            dma((CHIPS,)),
            dma((CHIPS,)),
            dma((4,)),
            dma((4,)),
        ],
        compiler_params=pltpu.CompilerParams(
            has_side_effects=True, vmem_limit_bytes=48 * 2**20
        ),
    )(tenants, inputs, grad_out, base_weight, adapter_a, adapter_b, magnitude)


def solution(mesh):
    return jax.shard_map(
        local,
        mesh=mesh,
        in_specs=(
            P(None, None, "tensor"),
            P(None, None, "tensor"),
            P(),
            P("section", None, "tensor"),
            P("section", None, None, None),
            P("section", None, None, "tensor"),
            P("section", None, "tensor"),
        ),
        out_specs=(
            P("section", None, None, "tensor"),
            P("section", None, None, "tensor"),
            P("section", None, "tensor"),
        ),
        check_vma=False,
    )
```

```python
import jax
import jax.numpy as jnp
from jax import lax
from jax.experimental import pallas as pl
from jax.experimental.pallas import tpu as pltpu
from jax.sharding import PartitionSpec as P

MESH = pl.DeviceIdType.MESH
F32 = jnp.float32
BF16 = jnp.bfloat16
HIGHEST = lax.Precision.HIGHEST

L = 4
TOK = 128
NH = 2
H = TOK // NH
D = 4096
R = 16
COLS = 128
CHIPS = 16
EXT = 16
RSB = H + EXT
HALF = D // 2
WCH = 8
WROWS = HALF // WCH


def hops(r):
    dz, dy = divmod(r, 4)
    return min(dz, 4 - dz) + min(dy, 4 - dy)


NEAR = sorted(range(CHIPS), key=hops)
GROUPS = [(1, 4), (5, 6), (11, 5)]
QUADS = [12, 8, 4, 0]


def inverse(p):
    dz, dy = divmod(NEAR[p], 4)
    return NEAR.index(((4 - dz) % 4) * 4 + (4 - dy) % 4)


def dot(a, b, ca, cb, precision=None):
    return lax.dot_general(
        a, b, (((ca,), (cb,)), ((), ())), precision=precision, preferred_element_type=F32
    )


def split3(v):
    hi = v.astype(BF16)
    rest = v - hi.astype(F32)
    mid = rest.astype(BF16)
    low = (rest - mid.astype(F32)).astype(BF16)
    return jnp.concatenate([hi, mid, low], axis=0)


def fold3(v):
    return v[0:R] + v[R : 2 * R] + v[2 * R : 3 * R]


def kernel(
    ten_ref, x_hbm, g_hbm, w_hbm, a_hbm, b_hbm, m_hbm,
    oa_ref, ob_ref, om_ref,
    w_buf, a_own, b_own, m_own, sm_src, mg_src, sm_buf, mg_buf, ag_a, xg, cur, grad,
    sv_branch, sv_low, sv_root, sv_norm, sv_scale,
    cs_src, cs_dst, ce_src, ce_dst, rs_src, rs_dst, own_sum, own_ext, lx_src, lx_dst, ex_src, ex_dst,
    res, od_src, od_dst,
    loc_sem, w_send, w_recv, sm_send, sm_recv, mg_send, mg_recv,
    aa_send, aa_recv, ac_send, ac_recv,
    ag_send, ag_recv, cf_send, cf_recv,
    cs_send, cs_recv, ce_send, ce_recv, rs_send, rs_recv,
    lx_send, lx_recv, ex_send, ex_recv, od_send, od_recv,
):
    s = lax.axis_index("section")
    t = lax.axis_index("tensor")
    z = t // 8
    y = (t // 2) % 4
    c = t % 2

    def plane(p):
        dz, dy = divmod(NEAR[p], 4)
        return (s, ((z + dz) % 4) * 8 + ((y + dy) % 4) * 2 + c)

    def source(p):
        dz, dy = divmod(NEAR[p], 4)
        return ((z + 4 - dz) % 4) * 4 + (y + 4 - dy) % 4

    partner = (s, t + 1 - 2 * c)

    def section(d):
        return ((s + d) % 4, t)

    def remote(src, dst, send, recv, device):
        return pltpu.make_async_remote_copy(
            src_ref=src, dst_ref=dst, send_sem=send, recv_sem=recv,
            device_id=device, device_id_type=MESH,
        )

    def every(n, fn):
        lax.fori_loop(0, n, lambda i, _: (fn(i), 0)[1], 0)

    def w_copy(layer, way, j, from_hbm=False):
        rows = pl.ds(way * HALF + j * WROWS, WROWS)
        src = w_hbm.at[0, rows] if from_hbm else w_buf.at[layer, rows]
        return remote(
            src, w_buf.at[layer, rows], w_send.at[layer, way, j], w_recv.at[layer, way, j],
            section(1 + 2 * way),
        )

    def sm_copy(d):
        return remote(sm_src.at[d], sm_buf.at[s], sm_send.at[d], sm_recv.at[d], section(d))

    def mg_copy(d):
        return remote(mg_src.at[d], mg_buf.at[s], mg_send.at[d], mg_recv.at[d], section(d))

    def aa_copy(p, g):
        return remote(ag_a.at[c, 0], ag_a.at[c, p], aa_send, aa_recv.at[g], plane(p))

    def aa_all(first, n, g):
        part = ag_a.at[c, pl.ds(first, n)]
        return remote(part, part, aa_send, aa_recv.at[g], partner)

    def ac_copy(core):
        return remote(ag_a.at[core], ag_a.at[core], ac_send, ac_recv, partner)

    def ag_copy(l, h, p, g):
        return remote(
            xg.at[l, h, c, 0], xg.at[l, h, c, p], ag_send.at[l, h], ag_recv.at[l, h, g], plane(p)
        )

    def ag_all(l, h, first, n, g):
        part = xg.at[l, h, c, pl.ds(first, n)]
        return remote(part, part, ag_send.at[l, h], ag_recv.at[l, h, g], partner)

    def cf_copy(l, h, first, n, g, core):
        part = xg.at[l, h, core, pl.ds(first, n)]
        return remote(part, part, cf_send.at[l, h, g], cf_recv.at[l, h, g], partner)

    def cs_copy(l, h, q):
        part = pl.ds(QUADS[q], 4)
        return remote(
            cs_src.at[l, h, part], cs_dst.at[l, h, part],
            cs_send.at[l, h, q], cs_recv.at[l, h, q], partner,
        )

    def ce_copy(l, h):
        return remote(
            ce_src.at[l, h], ce_dst.at[l, h], ce_send.at[l, h], ce_recv.at[l, h], partner
        )

    def rs_copy(l, h, p, g):
        return remote(
            rs_src.at[l, h, p], rs_dst.at[l, h, p], rs_send.at[l, h], rs_recv.at[l, h, g], plane(p)
        )

    def rs_all(l, h, first, n, g):
        part = pl.ds(first, n)
        return remote(
            rs_src.at[l, h, part], rs_dst.at[l, h, part],
            rs_send.at[l, h], rs_recv.at[l, h, g], partner,
        )

    def lx_copy():
        return remote(lx_src, lx_dst, lx_send, lx_recv, partner)

    def ex_copy(p):
        return remote(ex_src, ex_dst.at[p], ex_send, ex_recv, plane(p))

    def ex_all():
        part = ex_dst.at[pl.ds(1, CHIPS - 1)]
        return remote(part, part, ex_send, ex_recv, partner)

    def od_copy(d):
        return remote(
            od_src.at[(s + d) % 4], od_dst.at[s], od_send.at[d], od_recv.at[d], section(d)
        )

    def group_of(p):
        return [g for g, (first, n) in enumerate(GROUPS) if first <= p < first + n][0]

    own_x = pltpu.make_async_copy(x_hbm.at[s], cur, loc_sem.at[0])
    own_x.start()
    own_a = pltpu.make_async_copy(
        a_hbm.at[0, :, :, pl.ds(pl.multiple_of(t * COLS, COLS), COLS)], a_own, loc_sem.at[1]
    )
    own_a.start()
    own_b = pltpu.make_async_copy(b_hbm.at[0], b_own, loc_sem.at[2])
    own_b.start()
    own_m = pltpu.make_async_copy(m_hbm.at[0], m_own, loc_sem.at[3])
    own_m.start()
    own_w = pltpu.make_async_copy(w_hbm.at[0], w_buf.at[s], loc_sem.at[4])
    own_w.start()
    own_g = pltpu.make_async_copy(g_hbm.at[s], grad, loc_sem.at[5])
    own_g.start()

    def pick(values):
        out = jnp.int32(values[3])
        for i in range(3):
            out = jnp.where(s == i, jnp.int32(values[i]), out)
        return out

    def leave_own(way, cond):
        @pl.when(cond)
        def _():
            every(WCH, lambda j: w_copy(s, way, j, True).start())

    def pass_on(layer, way, j):
        w_copy(layer, way, j).wait_recv()
        w_copy(layer, way, j).start()

    leave_own(0, (s == 0) | (s == 3))
    leave_own(1, (s == 0) | (s == 1))

    own_x.wait()

    def send_block(l, h):
        xg[l, h, c, 0] = cur[h * H : (h + 1) * H]
        for p in reversed(range(1, CHIPS)):
            ag_copy(l, h, p, group_of(p)).start()
        cf_copy(l, h, 0, 1, 3, c).start()

    for h in range(NH):
        send_block(0, h)

    own_a.wait()
    own_b.wait()
    own_m.wait()
    for d in range(4):
        tenant = ten_ref[(s + d) % 4]
        pair = jnp.concatenate([a_own[tenant], b_own[tenant]], axis=0)
        mag = jnp.broadcast_to(m_own[pl.ds(tenant, 1), :], (8, COLS))
        if d == 0:
            sm_buf[s] = pair
            mg_buf[s] = mag
        else:
            sm_src[d] = pair
            mg_src[d] = mag
            sm_copy(d).start()
            mg_copy(d).start()
    for d in range(1, 4):
        sm_copy(d).wait_recv()
        mg_copy(d).wait_recv()
    for l in range(L):
        ag_a[c, 0, l * R : (l + 1) * R] = sm_buf[l, 0:R]
    for p in reversed(range(1, CHIPS)):
        aa_copy(p, group_of(p)).start()

    def round0(j):
        @pl.when((s == 1) | (s == 2))
        def _():
            pass_on(0, 0, j)

        @pl.when((s == 3) | (s == 2))
        def _():
            pass_on(0, 1, j)

    every(WCH, round0)
    own_w.wait()

    leave_own(0, s == 1)
    leave_own(1, s == 2)

    def round1_early(j):
        @pl.when(s == 0)
        def _():
            pass_on(3, 0, j)
            pass_on(1, 1, j)

    every(WCH, round1_early)

    for g, (first, n) in enumerate(GROUPS):
        aa_all(first, n, g).wait_recv()
    ac_copy(c).start()
    ac_copy(1 - c).wait_recv()

    def round1_late(j):
        @pl.when((s == 2) | (s == 3))
        def _():
            pass_on(1, 0, j)

        @pl.when((s == 1) | (s == 3))
        def _():
            pass_on(pick((0, 2, 0, 1)), 1, j)

    def round2_early(j):
        @pl.when(s == 1)
        def _():
            pass_on(3, 0, j)

        @pl.when(s == 0)
        def _():
            pass_on(2, 1, j)

    def round2_late(j):
        @pl.when((s == 3) | (s == 0))
        def _():
            pass_on(2, 0, j)

        @pl.when((s == 2) | (s == 1))
        def _():
            pass_on(3, 1, j)

    def a_rows(l, p):
        rows = pl.ds(pl.multiple_of(l * R, R), R)
        return jnp.concatenate([ag_a[0, p, rows, :], ag_a[1, p, rows, :]], axis=1)

    def w_rows(l, p):
        return w_buf[l, pl.ds(pl.multiple_of(source(p) * 256, 256), 256), :]

    def column_norms(l):
        def squares(i, total):
            rows = w_buf[l, pl.ds(pl.multiple_of(i * 256, 256), 256), :].astype(F32)
            return total + jnp.sum((rows * rows).reshape(32, 8, COLS), axis=0)

        base_sq = jnp.sum(
            lax.fori_loop(0, 16, squares, jnp.zeros((8, COLS), F32)), axis=0, keepdims=True
        )
        cross = jnp.zeros((R, COLS), F32)
        gram = jnp.zeros((R, R), F32)
        for p in range(CHIPS):
            a_p = a_rows(l, p)
            cross = cross + dot(a_p, w_rows(l, p), 1, 0)
            gram = gram + dot(a_p, a_p, 1, 1)
        b_wide = sm_buf[l, R : 2 * R].astype(F32)
        quad = dot(gram, b_wide, 1, 0, HIGHEST)
        total = base_sq + jnp.sum(b_wide * (2.0 * cross + quad), axis=0, keepdims=True)
        norm = jnp.sqrt(total + 1e-06)
        sv_norm[l] = jnp.broadcast_to(norm, (8, COLS))
        sv_scale[l] = jnp.broadcast_to(mg_buf[l, 0:1] / norm, (8, COLS))

    def forward(l, _):
        @pl.when(l == 1)
        def _():
            every(WCH, round1_late)
            leave_own(0, s == 2)
            leave_own(1, s == 3)
            every(WCH, round2_early)

        @pl.when(l == 2)
        def _():
            every(WCH, round2_late)

        @pl.when((s + 1) % 4 == l)
        def _():
            every(WCH, lambda j: w_copy(l, 0, j).wait_recv())

        @pl.when((s + 3) % 4 == l)
        def _():
            every(WCH, lambda j: w_copy(l, 1, j).wait_recv())

        column_norms(l)
        for h in range(NH):
            tokens = slice(h * H, (h + 1) * H)
            acc = jnp.zeros((H, COLS), F32)
            low_acc = jnp.zeros((H, R), F32)
            ssq = jnp.zeros((H, COLS), F32)

            def use(first, n, g, acc, low_acc, ssq):
                cf_copy(l, h, first, n, g, 1 - c).wait_recv()
                for p in range(first, first + n):
                    both = jnp.concatenate([xg[l, h, 0, p], xg[l, h, 1, p]], axis=1)
                    acc = acc + dot(both, w_rows(l, p), 1, 0)
                    low_acc = low_acc + dot(both, a_rows(l, p), 1, 1)
                    wide = both.astype(F32)
                    wide = wide * wide
                    ssq = ssq + wide[:, 0:COLS] + wide[:, COLS:]
                return acc, low_acc, ssq

            before = (0, 1, 3)
            for g, (first, n) in enumerate(GROUPS):
                ag_all(l, h, first, n, g).wait_recv()
                cf_copy(l, h, first, n, g, c).start()
                acc, low_acc, ssq = use(*before, acc, low_acc, ssq)
                before = (first, n, g)
            acc, low_acc, ssq = use(*before, acc, low_acc, ssq)

            mean = jnp.sum(ssq, axis=1, keepdims=True) * (1.0 / D)
            root = jnp.sqrt(mean + 1e-05)
            inv = 1.0 / root
            low = (low_acc * inv).astype(BF16)
            branch = acc * inv + dot(low, sm_buf[l, R : 2 * R], 1, 0)
            sv_branch[l, tokens] = branch
            sv_low[l, tokens] = low
            sv_root[l, tokens] = jnp.broadcast_to(root, (H, COLS))
            state = cur[tokens].astype(F32) + sv_scale[l, 0:1] * branch
            cur[tokens] = state.astype(BF16)

            @pl.when(l < L - 1)
            def _():
                send_block(l + 1, h)

        return 0

    lax.fori_loop(0, L, forward, 0)

    own_g.wait()

    def local_grads(l, h0, h1, first):
        tokens = slice(h0, h1)
        up = grad[tokens].astype(F32)
        branch = sv_branch[l, tokens]
        grad_branch = (up * sv_scale[l, 0:1]).astype(BF16)
        gm = jnp.sum(up * branch, axis=0, keepdims=True) / sv_norm[l, 0:1]
        gm = jnp.broadcast_to(gm, (8, COLS))
        gb = dot(sv_low[l, tokens], grad_branch, 0, 0)
        if not first:
            gb = gb + res[l, R : 2 * R]
            gm = gm + res[l, 2 * R : 2 * R + 8]
        res[l, R : 2 * R] = gb
        res[l, 2 * R : 2 * R + 8] = gm
        rank_t = dot(sm_buf[l, R : 2 * R], grad_branch, 1, 1)
        return branch, grad_branch, rank_t

    def begin(l, h):
        tokens = slice(h * H, (h + 1) * H)
        branch, grad_branch, rank_t = local_grads(l, h * H, (h + 1) * H, h == 0)
        prod = grad_branch.astype(F32) * branch * sv_root[l, tokens]
        row = jnp.sum(prod.T, axis=0, keepdims=True)
        row = jnp.concatenate([row, jnp.zeros((1, COLS - H), F32)], axis=1)
        ce_src[l, h] = jnp.concatenate(
            [
                jnp.concatenate([rank_t[0:8], rank_t[8:16]], axis=1),
                jnp.broadcast_to(row, (8, COLS)),
            ],
            axis=0,
        )
        ce_copy(l, h).start()
        rank = rank_t.T
        rank_hi = rank.astype(BF16)
        rank_lo = (rank - rank_hi.astype(F32)).astype(BF16)
        rank_two = jnp.concatenate([rank_hi, rank_lo], axis=1)

        def part(p, core):
            q = inverse(p)
            start = pl.multiple_of(source(q) * 256 + core * COLS, COLS)
            rows = w_buf[l, pl.ds(start, COLS), :]
            a_q = ag_a[core, q, pl.ds(pl.multiple_of(l * R, R), R), :]
            return dot(grad_branch, rows, 1, 1) + dot(
                rank_two, jnp.concatenate([a_q, a_q], axis=0), 1, 0
            )

        def away(q):
            for p in range(QUADS[q], QUADS[q] + 4):
                cs_src[l, h, p] = part(p, 1 - c).astype(BF16)
            cs_copy(l, h, q).start()

        away(0)
        away(1)
        ext_b = None
        for q in range(4):
            if q < 2:
                away(q + 2)
            mine = {p: part(p, c) for p in range(QUADS[q], QUADS[q] + 4)}
            if q == 0:
                ce_copy(l, h).wait_recv()
                ext = ce_src[l, h] + ce_dst[l, h]
                row = ext[8:16, 0:H]
                row_hi = row.astype(BF16).astype(F32)
                ext = jnp.concatenate(
                    [ext[0:8], jnp.concatenate([row_hi, row - row_hi], axis=1)], axis=0
                )
                own_ext[h] = ext
                ext_b = ext.astype(BF16)
            cs_copy(l, h, q).wait_recv()
            for p in reversed(range(QUADS[q], QUADS[q] + 4)):
                total = mine[p] + cs_dst[l, h, p].astype(F32)
                if p:
                    rs_src[l, h, p, 0:H] = total.astype(BF16)
                    rs_src[l, h, p, H:RSB] = ext_b
                    rs_copy(l, h, p, group_of(p)).start()
                else:
                    own_sum[h] = total

    def adapter_grad(l, h0, h1, rank_sum, first):
        tokens = slice(h0, h1)
        if h1 - h0 == TOK:
            x_own = jnp.concatenate([xg[l, i, c, 0] for i in range(NH)], axis=0)
        else:
            x_own = xg[l, h0 // H, c, 0]
        normed = (x_own.astype(F32) / sv_root[l, tokens]).astype(BF16)
        ga = fold3(dot(split3(rank_sum), normed, 1, 0))
        if not first:
            ga = ga + res[l, 0:R]
        res[l, 0:R] = ga

    def finish(l, h):
        tokens = slice(h * H, (h + 1) * H)
        total = jnp.concatenate([own_sum[h], own_ext[h]], axis=0)
        for g, (first, n) in enumerate(GROUPS):
            rs_all(l, h, first, n, g).wait_recv()
            for p in range(first, first + n):
                total = total + rs_dst[l, h, p].astype(F32)
        grad_h = total[0:H]
        rank = total[H : H + 8]
        rank_sum = jnp.concatenate([rank[:, 0:H], rank[:, H:]], axis=0)
        row = total[H + 8 : H + 9]
        row = row[:, 0:H] + row[:, H:]
        row_dot = jnp.broadcast_to(row, (COLS, H)).T
        up = grad[tokens].astype(F32)
        x_own = xg[l, h, c, 0].astype(F32)
        inv = 1.0 / sv_root[l, tokens]
        state = up + (grad_h - x_own * (row_dot * (inv * inv) * (1.0 / D))) * inv
        grad[tokens] = state.astype(BF16)
        return rank_sum

    for h in range(NH):
        begin(L - 1, h)

    def backward(i, _):
        l = L - 1 - i
        for h in range(NH):
            rank_sum = finish(l, h)

            @pl.when(l > 1)
            def _():
                begin(l - 1, h)

            adapter_grad(l, h * H, (h + 1) * H, rank_sum, h == 0)
        return 0

    lax.fori_loop(0, L - 1, backward, 0)

    _, _, rank_t = local_grads(0, 0, TOK, True)
    sum_a = jnp.zeros((1, COLS), F32)
    sum_b = jnp.zeros((1, COLS), F32)
    sum_m = jnp.zeros((1, COLS), F32)
    for l in range(L):
        if l:
            ga = res[l, 0:R]
            sum_a = sum_a + jnp.sum(ga * ga, axis=0, keepdims=True)
        gb = res[l, R : 2 * R]
        sum_b = sum_b + jnp.sum(gb * gb, axis=0, keepdims=True)
        gm = res[l, 2 * R : 2 * R + 1]
        sum_m = sum_m + gm * gm
    lx_src[...] = jnp.concatenate(
        [rank_t, sum_a, sum_b, sum_m, jnp.zeros((5, COLS), F32)], axis=0
    )
    lx_copy().start()
    lx_copy().wait_recv()
    ext = lx_src[...] + lx_dst[...]
    ex_src[...] = ext
    for p in reversed(range(1, CHIPS)):
        ex_copy(p).start()
    outer = jnp.zeros((TOK, TOK), F32)
    for p in range(CHIPS):
        both = jnp.concatenate(
            [
                jnp.concatenate([xg[0, h, 0, p], xg[0, h, 1, p]], axis=1)
                for h in range(NH)
            ],
            axis=0,
        )
        outer = outer + dot(both, both, 1, 1)
    inv = 1.0 / sv_root[0]
    outer = outer * inv * inv.T
    ex_all().wait_recv()
    for p in range(1, CHIPS):
        ext = ext + ex_dst[p]
    rank_sum = ext[0:R]
    adapter_grad(0, 0, TOK, rank_sum, True)
    sq = rank_sum * dot(rank_sum, outer, 1, 0, HIGHEST)

    def norm_of(v, count):
        return 1.0 / jnp.sqrt(jnp.sum(v, axis=1, keepdims=True) * (1.0 / count) + 1e-06)

    by_a = norm_of(ext[R : R + 1] + jnp.sum(sq, axis=0, keepdims=True), L * R * D)
    by_b = norm_of(ext[R + 1 : R + 2], L * R * D)
    by_m = norm_of(ext[R + 2 : R + 3], L * D)
    for l in range(L):
        od_src[l, 0:R] = res[l, 0:R] * by_a
        od_src[l, R : 2 * R] = res[l, R : 2 * R] * by_b
        od_src[l, 2 * R : 2 * R + 8] = res[l, 2 * R : 2 * R + 8] * by_m
    for d in (2, 1, 3):
        od_copy(d).start()
    od_dst[s] = od_src[s]

    def drain_w(j):
        for h in range(3):
            w_copy((s + 4 - h) % 4, 0, j).wait_send()
            w_copy((s + h) % 4, 1, j).wait_send()

    every(WCH, drain_w)
    aa_all(1, CHIPS - 1, 0).wait_send()
    ac_copy(c).wait_send()

    def drain_l(l):
        for h in range(NH):
            ag_all(l, h, 1, CHIPS - 1, 0).wait_send()
            cf_copy(l, h, 0, 1, 3, c).wait_send()
            for g, (first, n) in enumerate(GROUPS):
                cf_copy(l, h, first, n, g, c).wait_send()

    every(L, drain_l)

    def drain_b(i):
        l = i + 1
        for h in range(NH):
            rs_all(l, h, 1, CHIPS - 1, 0).wait_send()
            ce_copy(l, h).wait_send()
            for q in range(4):
                cs_copy(l, h, q).wait_send()

    every(L - 1, drain_b)
    lx_copy().wait_send()
    ex_all().wait_send()
    for d in range(1, 4):
        sm_copy(d).wait_send()
        mg_copy(d).wait_send()

    for d in (1, 3, 2):
        od_copy(d).wait_recv()
    for tenant in range(4):
        out = jnp.zeros((2 * R + 8, COLS), F32)
        for k in range(4):
            out = jnp.where(ten_ref[k] == tenant, od_dst[k], out)
        oa_ref[0, tenant] = out[0:R]
        ob_ref[0, tenant] = out[R : 2 * R]
        om_ref[0, pl.ds(tenant, 1), :] = out[2 * R : 2 * R + 1]
    for d in range(1, 4):
        od_copy(d).wait_send()


def local(inputs, grad_out, tenants, base_weight, adapter_a, adapter_b, magnitude):
    vmem = pl.BlockSpec(memory_space=pltpu.VMEM)
    hbm = pl.BlockSpec(memory_space=pl.ANY)
    dma = pltpu.SemaphoreType.DMA
    return pl.pallas_call(
        kernel,
        out_shape=(
            jax.ShapeDtypeStruct((1, 4, R, COLS), F32),
            jax.ShapeDtypeStruct((1, 4, R, COLS), F32),
            jax.ShapeDtypeStruct((1, 4, COLS), F32),
        ),
        in_specs=[pl.BlockSpec(memory_space=pltpu.SMEM)] + [hbm] * 6,
        out_specs=(vmem, vmem, vmem),
        scratch_shapes=[
            pltpu.VMEM((L, D, COLS), BF16),
            pltpu.VMEM((4, R, COLS), BF16),
            pltpu.VMEM((4, R, COLS), BF16),
            pltpu.VMEM((4, COLS), F32),
            pltpu.VMEM((4, 2 * R, COLS), BF16),
            pltpu.VMEM((4, 8, COLS), F32),
            pltpu.VMEM((4, 2 * R, COLS), BF16),
            pltpu.VMEM((4, 8, COLS), F32),
            pltpu.VMEM((2, CHIPS, L * R, COLS), BF16),
            pltpu.VMEM((L, NH, 2, CHIPS, H, COLS), BF16),
            pltpu.VMEM((TOK, COLS), BF16),
            pltpu.VMEM((TOK, COLS), BF16),
            pltpu.VMEM((L, TOK, COLS), F32),
            pltpu.VMEM((L, TOK, R), BF16),
            pltpu.VMEM((L, TOK, COLS), F32),
            pltpu.VMEM((L, 8, COLS), F32),
            pltpu.VMEM((L, 8, COLS), F32),
            pltpu.VMEM((L, NH, CHIPS, H, COLS), BF16),
            pltpu.VMEM((L, NH, CHIPS, H, COLS), BF16),
            pltpu.VMEM((L, NH, EXT, COLS), F32),
            pltpu.VMEM((L, NH, EXT, COLS), F32),
            pltpu.VMEM((L, NH, CHIPS, RSB, COLS), BF16),
            pltpu.VMEM((L, NH, CHIPS, RSB, COLS), BF16),
            pltpu.VMEM((NH, H, COLS), F32),
            pltpu.VMEM((NH, EXT, COLS), F32),
            pltpu.VMEM((R + 8, TOK), F32),
            pltpu.VMEM((R + 8, TOK), F32),
            pltpu.VMEM((R + 8, TOK), F32),
            pltpu.VMEM((CHIPS, R + 8, TOK), F32),
            pltpu.VMEM((L, 2 * R + 8, COLS), F32),
            pltpu.VMEM((L, 2 * R + 8, COLS), F32),
            pltpu.VMEM((L, 2 * R + 8, COLS), F32),
            dma((6,)),
            dma((L, 2, WCH)),
            dma((L, 2, WCH)),
            dma((4,)),
            dma((4,)),
            dma((4,)),
            dma((4,)),
            dma,
            dma((3,)),
            dma,
            dma,
            dma((L, NH)),
            dma((L, NH, 3)),
            dma((L, NH, 4)),
            dma((L, NH, 4)),
            dma((L, NH, 4)),
            dma((L, NH, 4)),
            dma((L, NH)),
            dma((L, NH)),
            dma((L, NH)),
            dma((L, NH, 3)),
            dma,
            dma,
            dma,
            dma,
            dma((4,)),
            dma((4,)),
        ],
        compiler_params=pltpu.CompilerParams(
            has_side_effects=True, vmem_limit_bytes=60 * 2**20
        ),
    )(tenants, inputs, grad_out, base_weight, adapter_a, adapter_b, magnitude)


def solution(mesh):
    return jax.shard_map(
        local,
        mesh=mesh,
        in_specs=(
            P(None, None, "tensor"),
            P(None, None, "tensor"),
            P(),
            P("section", None, "tensor"),
            P("section", None, None, None),
            P("section", None, None, "tensor"),
            P("section", None, "tensor"),
        ),
        out_specs=(
            P("section", None, None, "tensor"),
            P("section", None, None, "tensor"),
            P("section", None, "tensor"),
        ),
        check_vma=False,
    )
```

```python
import jax
import jax.numpy as jnp
from jax import lax
from jax.experimental import pallas as pl
from jax.experimental.pallas import tpu as pltpu
from jax.sharding import PartitionSpec as P

MESH = pl.DeviceIdType.MESH
F32 = jnp.float32
BF16 = jnp.bfloat16
HIGHEST = lax.Precision.HIGHEST

L = 4
TOK = 128
NH = 2
H = TOK // NH
D = 4096
R = 16
COLS = 128
CHIPS = 16
EXT = 16
RSB = H + EXT
HALF = D // 2
WCH = 8
WROWS = HALF // WCH


def hops(r):
    dz, dy = divmod(r, 4)
    return min(dz, 4 - dz) + min(dy, 4 - dy)


NEAR = sorted(range(CHIPS), key=hops)
GROUPS = [(1, 4), (5, 6), (11, 5)]
QUADS = [12, 8, 4, 0]


def inverse(p):
    dz, dy = divmod(NEAR[p], 4)
    return NEAR.index(((4 - dz) % 4) * 4 + (4 - dy) % 4)


def dot(a, b, ca, cb, precision=None):
    return lax.dot_general(
        a, b, (((ca,), (cb,)), ((), ())), precision=precision, preferred_element_type=F32
    )


def split3(v):
    hi = v.astype(BF16)
    rest = v - hi.astype(F32)
    mid = rest.astype(BF16)
    low = (rest - mid.astype(F32)).astype(BF16)
    return jnp.concatenate([hi, mid, low], axis=0)


def fold3(v):
    return v[0:R] + v[R : 2 * R] + v[2 * R : 3 * R]


def kernel(
    ten_ref, x_hbm, g_hbm, w_hbm, a_hbm, b_hbm, m_hbm,
    oa_ref, ob_ref, om_ref,
    w_buf, a_own, b_own, m_own, sm_src, mg_src, sm_buf, mg_buf, ag_a, xg, cur, grad,
    sv_branch, sv_low, sv_root, sv_norm, sv_scale,
    cs_src, cs_dst, ce_src, ce_dst, rs_src, rs_dst, own_sum, own_ext, lx_src, lx_dst, ex_src, ex_dst,
    res, od_src, od_dst,
    loc_sem, w_send, w_recv, sm_send, sm_recv, mg_send, mg_recv,
    aa_send, aa_recv, ac_send, ac_recv,
    ag_send, ag_recv, cf_send, cf_recv,
    cs_send, cs_recv, ce_send, ce_recv, rs_send, rs_recv,
    lx_send, lx_recv, ex_send, ex_recv, od_send, od_recv,
):
    s = lax.axis_index("section")
    t = lax.axis_index("tensor")
    z = t // 8
    y = (t // 2) % 4
    c = t % 2

    def plane(p):
        dz, dy = divmod(NEAR[p], 4)
        return (s, ((z + dz) % 4) * 8 + ((y + dy) % 4) * 2 + c)

    def source(p):
        dz, dy = divmod(NEAR[p], 4)
        return ((z + 4 - dz) % 4) * 4 + (y + 4 - dy) % 4

    partner = (s, t + 1 - 2 * c)

    def section(d):
        return ((s + d) % 4, t)

    def remote(src, dst, send, recv, device):
        return pltpu.make_async_remote_copy(
            src_ref=src, dst_ref=dst, send_sem=send, recv_sem=recv,
            device_id=device, device_id_type=MESH,
        )

    def every(n, fn):
        lax.fori_loop(0, n, lambda i, _: (fn(i), 0)[1], 0)

    def w_own(way, half, j):
        rows = pl.ds(half * HALF + j * WROWS, WROWS)
        return remote(
            w_hbm.at[0, rows], w_buf.at[s, rows], w_send.at[0, way], w_recv.at[s, half, j],
            section(1 + 2 * way),
        )

    def w_pass(layer, half, j):
        rows = pl.ds(half * HALF + j * WROWS, WROWS)
        return remote(
            w_buf.at[layer, rows], w_buf.at[layer, rows], w_send.at[1, half],
            w_recv.at[layer, half, j], section(1 + 2 * half),
        )

    def w_left(kind, way, n):
        rows = pl.ds(0, n)
        return remote(
            w_hbm.at[0, rows], w_buf.at[s, rows], w_send.at[kind, way], w_recv.at[0, 0, 0],
            section(1),
        )

    def sm_copy(d):
        return remote(sm_src.at[d], sm_buf.at[s], sm_send.at[d], sm_recv.at[d], section(d))

    def mg_copy(d):
        return remote(mg_src.at[d], mg_buf.at[s], mg_send.at[d], mg_recv.at[d], section(d))

    def aa_copy(p, g):
        return remote(ag_a.at[c, 0], ag_a.at[c, p], aa_send, aa_recv.at[g], plane(p))

    def aa_all(first, n, g):
        part = ag_a.at[c, pl.ds(first, n)]
        return remote(part, part, aa_send, aa_recv.at[g], partner)

    def ac_copy(core):
        return remote(ag_a.at[core], ag_a.at[core], ac_send, ac_recv, partner)

    def ag_copy(l, h, p, g):
        return remote(
            xg.at[l, h, c, 0], xg.at[l, h, c, p], ag_send.at[l, h], ag_recv.at[l, h, g], plane(p)
        )

    def ag_all(l, h, first, n, g):
        part = xg.at[l, h, c, pl.ds(first, n)]
        return remote(part, part, ag_send.at[l, h], ag_recv.at[l, h, g], partner)

    def cf_copy(l, h, first, n, g, core):
        part = xg.at[l, h, core, pl.ds(first, n)]
        return remote(part, part, cf_send.at[l, h, g], cf_recv.at[l, h, g], partner)

    def cs_copy(l, h, q):
        part = pl.ds(QUADS[q], 4)
        return remote(
            cs_src.at[l, h, part], cs_dst.at[l, h, part],
            cs_send.at[l, h, q], cs_recv.at[l, h, q], partner,
        )

    def ce_copy(l, h):
        return remote(
            ce_src.at[l, h], ce_dst.at[l, h], ce_send.at[l, h], ce_recv.at[l, h], partner
        )

    def rs_copy(l, h, p, g):
        return remote(
            rs_src.at[l, h, p], rs_dst.at[l, h, p], rs_send.at[l, h], rs_recv.at[l, h, g], plane(p)
        )

    def rs_all(l, h, first, n, g):
        part = pl.ds(first, n)
        return remote(
            rs_src.at[l, h, part], rs_dst.at[l, h, part],
            rs_send.at[l, h], rs_recv.at[l, h, g], partner,
        )

    def lx_copy():
        return remote(lx_src, lx_dst, lx_send, lx_recv, partner)

    def ex_copy(p):
        return remote(ex_src, ex_dst.at[p], ex_send, ex_recv, plane(p))

    def ex_all():
        part = ex_dst.at[pl.ds(1, CHIPS - 1)]
        return remote(part, part, ex_send, ex_recv, partner)

    def od_copy(d):
        return remote(
            od_src.at[(s + d) % 4], od_dst.at[s], od_send.at[d], od_recv.at[d], section(d)
        )

    def group_of(p):
        return [g for g, (first, n) in enumerate(GROUPS) if first <= p < first + n][0]

    own_x = pltpu.make_async_copy(x_hbm.at[s], cur, loc_sem.at[0])
    own_x.start()
    own_a = pltpu.make_async_copy(
        a_hbm.at[0, :, :, pl.ds(pl.multiple_of(t * COLS, COLS), COLS)], a_own, loc_sem.at[1]
    )
    own_a.start()
    own_b = pltpu.make_async_copy(b_hbm.at[0], b_own, loc_sem.at[2])
    own_b.start()
    own_m = pltpu.make_async_copy(m_hbm.at[0], m_own, loc_sem.at[3])
    own_m.start()
    own_w = pltpu.make_async_copy(w_hbm.at[0], w_buf.at[s], loc_sem.at[4])
    own_w.start()
    own_g = pltpu.make_async_copy(g_hbm.at[s], grad, loc_sem.at[5])
    own_g.start()

    barrier = pltpu.get_barrier_semaphore()
    peers = [plane(p) for p in range(1, CHIPS)] + [section(d) for d in (1, 2, 3)] + [partner]
    for peer in peers:
        pl.semaphore_signal(barrier, inc=1, device_id=peer, device_id_type=MESH)
    own_a.wait()
    own_b.wait()
    own_m.wait()
    for d in range(4):
        tenant = ten_ref[(s + d) % 4]
        pair = jnp.concatenate([a_own[tenant], b_own[tenant]], axis=0)
        mag = jnp.broadcast_to(m_own[pl.ds(tenant, 1), :], (8, COLS))
        if d == 0:
            sm_buf[s] = pair
            mg_buf[s] = mag
        else:
            sm_src[d] = pair
            mg_src[d] = mag
    own_x.wait()

    pl.semaphore_wait(barrier, len(peers))

    for d in (2, 1, 3):
        sm_copy(d).start()
        mg_copy(d).start()

    def send_block(l, h):
        xg[l, h, c, 0] = cur[h * H : (h + 1) * H]
        for p in reversed(range(1, CHIPS)):
            ag_copy(l, h, p, group_of(p)).start()
        cf_copy(l, h, 0, 1, 3, c).start()

    def send_own(way):
        for half in (way, 1 - way):
            every(WCH, lambda j: w_own(way, half, j).start())

    def pass_on(layer, half):
        def one(j):
            w_pass(layer, half, j).wait_recv()
            w_pass(layer, half, j).start()

        every(WCH, one)

    @pl.when(s != 1)
    def _():
        send_own(0)

    @pl.when(s != 3)
    def _():
        send_own(1)

    for h in range(NH):
        send_block(0, h)
    for d in range(1, 4):
        sm_copy(d).wait_recv()
        mg_copy(d).wait_recv()
    for l in range(L):
        ag_a[c, 0, l * R : (l + 1) * R] = sm_buf[l, 0:R]
    for p in reversed(range(1, CHIPS)):
        aa_copy(p, group_of(p)).start()

    @pl.when(s == 1)
    def _():
        pass_on(0, 0)
        send_own(0)
        w_left(0, 1, D).wait_send()
        pass_on(2, 1)

    @pl.when(s == 3)
    def _():
        pass_on(0, 1)
        send_own(1)
        w_left(0, 0, D).wait_send()
        pass_on(2, 0)

    own_w.wait()

    for g, (first, n) in enumerate(GROUPS):
        aa_all(first, n, g).wait_recv()
    ac_copy(c).start()
    ac_copy(1 - c).wait_recv()

    def pass_late():
        @pl.when((s == 0) | (s == 2))
        def _():
            w_left(0, 0, D).wait_send()
            w_left(0, 1, D).wait_send()
            pass_on((s + 3) % 4, 0)
            pass_on((s + 1) % 4, 1)

    def a_rows(l, p):
        rows = pl.ds(pl.multiple_of(l * R, R), R)
        return jnp.concatenate([ag_a[0, p, rows, :], ag_a[1, p, rows, :]], axis=1)

    def w_rows(l, p):
        return w_buf[l, pl.ds(pl.multiple_of(source(p) * 256, 256), 256), :]

    def column_norms(l):
        def squares(i, total):
            rows = w_buf[l, pl.ds(pl.multiple_of(i * 256, 256), 256), :].astype(F32)
            return total + jnp.sum((rows * rows).reshape(32, 8, COLS), axis=0)

        base_sq = jnp.sum(
            lax.fori_loop(0, 16, squares, jnp.zeros((8, COLS), F32)), axis=0, keepdims=True
        )
        cross = jnp.zeros((R, COLS), F32)
        gram = jnp.zeros((R, R), F32)
        for p in range(CHIPS):
            a_p = a_rows(l, p)
            cross = cross + dot(a_p, w_rows(l, p), 1, 0)
            gram = gram + dot(a_p, a_p, 1, 1)
        b_wide = sm_buf[l, R : 2 * R].astype(F32)
        quad = dot(gram, b_wide, 1, 0, HIGHEST)
        total = base_sq + jnp.sum(b_wide * (2.0 * cross + quad), axis=0, keepdims=True)
        norm = jnp.sqrt(total + 1e-06)
        sv_norm[l] = jnp.broadcast_to(norm, (8, COLS))
        sv_scale[l] = jnp.broadcast_to(mg_buf[l, 0:1] / norm, (8, COLS))

    def forward(l, _):
        @pl.when(l == 1)
        def _():
            pass_late()

        behind = (s + 4 - l) % 4

        @pl.when(behind >= 2)
        def _():
            every(WCH, lambda j: w_pass(l, 0, j).wait_recv())

        @pl.when((behind == 1) | (behind == 2))
        def _():
            every(WCH, lambda j: w_pass(l, 1, j).wait_recv())

        column_norms(l)
        for h in range(NH):
            tokens = slice(h * H, (h + 1) * H)
            acc = jnp.zeros((H, COLS), F32)
            low_acc = jnp.zeros((H, R), F32)
            ssq = jnp.zeros((H, COLS), F32)

            def use(first, n, g, acc, low_acc, ssq):
                cf_copy(l, h, first, n, g, 1 - c).wait_recv()
                for p in range(first, first + n):
                    both = jnp.concatenate([xg[l, h, 0, p], xg[l, h, 1, p]], axis=1)
                    acc = acc + dot(both, w_rows(l, p), 1, 0)
                    low_acc = low_acc + dot(both, a_rows(l, p), 1, 1)
                    wide = both.astype(F32)
                    wide = wide * wide
                    ssq = ssq + wide[:, 0:COLS] + wide[:, COLS:]
                return acc, low_acc, ssq

            before = (0, 1, 3)
            for g, (first, n) in enumerate(GROUPS):
                ag_all(l, h, first, n, g).wait_recv()
                cf_copy(l, h, first, n, g, c).start()
                acc, low_acc, ssq = use(*before, acc, low_acc, ssq)
                before = (first, n, g)
            acc, low_acc, ssq = use(*before, acc, low_acc, ssq)

            mean = jnp.sum(ssq, axis=1, keepdims=True) * (1.0 / D)
            root = jnp.sqrt(mean + 1e-05)
            inv = 1.0 / root
            low = (low_acc * inv).astype(BF16)
            branch = acc * inv + dot(low, sm_buf[l, R : 2 * R], 1, 0)
            sv_branch[l, tokens] = branch
            sv_low[l, tokens] = low
            sv_root[l, tokens] = jnp.broadcast_to(root, (H, COLS))
            state = cur[tokens].astype(F32) + sv_scale[l, 0:1] * branch
            cur[tokens] = state.astype(BF16)

            @pl.when(l < L - 1)
            def _():
                send_block(l + 1, h)

        return 0

    lax.fori_loop(0, L, forward, 0)

    own_g.wait()

    def local_grads(l, h0, h1, first):
        tokens = slice(h0, h1)
        up = grad[tokens].astype(F32)
        branch = sv_branch[l, tokens]
        grad_branch = (up * sv_scale[l, 0:1]).astype(BF16)
        gm = jnp.sum(up * branch, axis=0, keepdims=True) / sv_norm[l, 0:1]
        gm = jnp.broadcast_to(gm, (8, COLS))
        gb = dot(sv_low[l, tokens], grad_branch, 0, 0)
        if not first:
            gb = gb + res[l, R : 2 * R]
            gm = gm + res[l, 2 * R : 2 * R + 8]
        res[l, R : 2 * R] = gb
        res[l, 2 * R : 2 * R + 8] = gm
        rank_t = dot(sm_buf[l, R : 2 * R], grad_branch, 1, 1)
        return branch, grad_branch, rank_t

    def begin(l, h):
        tokens = slice(h * H, (h + 1) * H)
        branch, grad_branch, rank_t = local_grads(l, h * H, (h + 1) * H, h == 0)
        prod = grad_branch.astype(F32) * branch * sv_root[l, tokens]
        row = jnp.sum(prod.T, axis=0, keepdims=True)
        row = jnp.concatenate([row, jnp.zeros((1, COLS - H), F32)], axis=1)
        ce_src[l, h] = jnp.concatenate(
            [
                jnp.concatenate([rank_t[0:8], rank_t[8:16]], axis=1),
                jnp.broadcast_to(row, (8, COLS)),
            ],
            axis=0,
        )
        ce_copy(l, h).start()
        rank = rank_t.T
        rank_hi = rank.astype(BF16)
        rank_lo = (rank - rank_hi.astype(F32)).astype(BF16)
        rank_two = jnp.concatenate([rank_hi, rank_lo], axis=1)

        def part(p, core):
            q = inverse(p)
            start = pl.multiple_of(source(q) * 256 + core * COLS, COLS)
            rows = w_buf[l, pl.ds(start, COLS), :]
            a_q = ag_a[core, q, pl.ds(pl.multiple_of(l * R, R), R), :]
            return dot(grad_branch, rows, 1, 1) + dot(
                rank_two, jnp.concatenate([a_q, a_q], axis=0), 1, 0
            )

        def away(q):
            for p in range(QUADS[q], QUADS[q] + 4):
                cs_src[l, h, p] = part(p, 1 - c).astype(BF16)
            cs_copy(l, h, q).start()

        away(0)
        away(1)
        ext_b = None
        for q in range(4):
            if q < 2:
                away(q + 2)
            mine = {p: part(p, c) for p in range(QUADS[q], QUADS[q] + 4)}
            if q == 0:
                ce_copy(l, h).wait_recv()
                ext = ce_src[l, h] + ce_dst[l, h]
                row = ext[8:16, 0:H]
                row_hi = row.astype(BF16).astype(F32)
                ext = jnp.concatenate(
                    [ext[0:8], jnp.concatenate([row_hi, row - row_hi], axis=1)], axis=0
                )
                own_ext[h] = ext
                ext_b = ext.astype(BF16)
            cs_copy(l, h, q).wait_recv()
            for p in reversed(range(QUADS[q], QUADS[q] + 4)):
                total = mine[p] + cs_dst[l, h, p].astype(F32)
                if p:
                    rs_src[l, h, p, 0:H] = total.astype(BF16)
                    rs_src[l, h, p, H:RSB] = ext_b
                    rs_copy(l, h, p, group_of(p)).start()
                else:
                    own_sum[h] = total

    def adapter_grad(l, h0, h1, rank_sum, first):
        tokens = slice(h0, h1)
        if h1 - h0 == TOK:
            x_own = jnp.concatenate([xg[l, i, c, 0] for i in range(NH)], axis=0)
        else:
            x_own = xg[l, h0 // H, c, 0]
        normed = (x_own.astype(F32) / sv_root[l, tokens]).astype(BF16)
        ga = fold3(dot(split3(rank_sum), normed, 1, 0))
        if not first:
            ga = ga + res[l, 0:R]
        res[l, 0:R] = ga

    def finish(l, h):
        tokens = slice(h * H, (h + 1) * H)
        total = jnp.concatenate([own_sum[h], own_ext[h]], axis=0)
        for g, (first, n) in enumerate(GROUPS):
            rs_all(l, h, first, n, g).wait_recv()
            for p in range(first, first + n):
                total = total + rs_dst[l, h, p].astype(F32)
        grad_h = total[0:H]
        rank = total[H : H + 8]
        rank_sum = jnp.concatenate([rank[:, 0:H], rank[:, H:]], axis=0)
        row = total[H + 8 : H + 9]
        row = row[:, 0:H] + row[:, H:]
        row_dot = jnp.broadcast_to(row, (COLS, H)).T
        up = grad[tokens].astype(F32)
        x_own = xg[l, h, c, 0].astype(F32)
        inv = 1.0 / sv_root[l, tokens]
        state = up + (grad_h - x_own * (row_dot * (inv * inv) * (1.0 / D))) * inv
        grad[tokens] = state.astype(BF16)
        return rank_sum

    for h in range(NH):
        begin(L - 1, h)

    def backward(i, _):
        l = L - 1 - i
        for h in range(NH):
            rank_sum = finish(l, h)

            @pl.when(l > 1)
            def _():
                begin(l - 1, h)

            adapter_grad(l, h * H, (h + 1) * H, rank_sum, h == 0)
        return 0

    lax.fori_loop(0, L - 1, backward, 0)

    _, _, rank_t = local_grads(0, 0, TOK, True)
    sum_a = jnp.zeros((1, COLS), F32)
    sum_b = jnp.zeros((1, COLS), F32)
    sum_m = jnp.zeros((1, COLS), F32)
    for l in range(L):
        if l:
            ga = res[l, 0:R]
            sum_a = sum_a + jnp.sum(ga * ga, axis=0, keepdims=True)
        gb = res[l, R : 2 * R]
        sum_b = sum_b + jnp.sum(gb * gb, axis=0, keepdims=True)
        gm = res[l, 2 * R : 2 * R + 1]
        sum_m = sum_m + gm * gm
    lx_src[...] = jnp.concatenate(
        [rank_t, sum_a, sum_b, sum_m, jnp.zeros((5, COLS), F32)], axis=0
    )
    lx_copy().start()
    lx_copy().wait_recv()
    ext = lx_src[...] + lx_dst[...]
    ex_src[...] = ext
    for p in reversed(range(1, CHIPS)):
        ex_copy(p).start()
    outer = jnp.zeros((TOK, TOK), F32)
    for p in range(CHIPS):
        both = jnp.concatenate(
            [
                jnp.concatenate([xg[0, h, 0, p], xg[0, h, 1, p]], axis=1)
                for h in range(NH)
            ],
            axis=0,
        )
        outer = outer + dot(both, both, 1, 1)
    inv = 1.0 / sv_root[0]
    outer = outer * inv * inv.T
    ex_all().wait_recv()
    for p in range(1, CHIPS):
        ext = ext + ex_dst[p]
    rank_sum = ext[0:R]
    adapter_grad(0, 0, TOK, rank_sum, True)
    sq = rank_sum * dot(rank_sum, outer, 1, 0, HIGHEST)

    def norm_of(v, count):
        return 1.0 / jnp.sqrt(jnp.sum(v, axis=1, keepdims=True) * (1.0 / count) + 1e-06)

    by_a = norm_of(ext[R : R + 1] + jnp.sum(sq, axis=0, keepdims=True), L * R * D)
    by_b = norm_of(ext[R + 1 : R + 2], L * R * D)
    by_m = norm_of(ext[R + 2 : R + 3], L * D)
    for l in range(L):
        od_src[l, 0:R] = res[l, 0:R] * by_a
        od_src[l, R : 2 * R] = res[l, R : 2 * R] * by_b
        od_src[l, 2 * R : 2 * R + 8] = res[l, 2 * R : 2 * R + 8] * by_m
    for d in (2, 1, 3):
        od_copy(d).start()
    od_dst[s] = od_src[s]

    @pl.when(s == 1)
    def _():
        w_left(0, 0, D).wait_send()

    @pl.when(s == 3)
    def _():
        w_left(0, 1, D).wait_send()

    w_left(1, 0, HALF).wait_send()
    w_left(1, 1, HALF).wait_send()
    aa_all(1, CHIPS - 1, 0).wait_send()
    ac_copy(c).wait_send()

    def drain_l(l):
        for h in range(NH):
            ag_all(l, h, 1, CHIPS - 1, 0).wait_send()
            cf_copy(l, h, 0, 1, 3, c).wait_send()
            for g, (first, n) in enumerate(GROUPS):
                cf_copy(l, h, first, n, g, c).wait_send()

    every(L, drain_l)

    def drain_b(i):
        l = i + 1
        for h in range(NH):
            rs_all(l, h, 1, CHIPS - 1, 0).wait_send()
            ce_copy(l, h).wait_send()
            for q in range(4):
                cs_copy(l, h, q).wait_send()

    every(L - 1, drain_b)
    lx_copy().wait_send()
    ex_all().wait_send()
    for d in range(1, 4):
        sm_copy(d).wait_send()
        mg_copy(d).wait_send()

    for d in (1, 3, 2):
        od_copy(d).wait_recv()
    for tenant in range(4):
        out = jnp.zeros((2 * R + 8, COLS), F32)
        for k in range(4):
            out = jnp.where(ten_ref[k] == tenant, od_dst[k], out)
        oa_ref[0, tenant] = out[0:R]
        ob_ref[0, tenant] = out[R : 2 * R]
        om_ref[0, pl.ds(tenant, 1), :] = out[2 * R : 2 * R + 1]
    for d in range(1, 4):
        od_copy(d).wait_send()


def local(inputs, grad_out, tenants, base_weight, adapter_a, adapter_b, magnitude):
    vmem = pl.BlockSpec(memory_space=pltpu.VMEM)
    hbm = pl.BlockSpec(memory_space=pl.ANY)
    dma = pltpu.SemaphoreType.DMA
    return pl.pallas_call(
        kernel,
        out_shape=(
            jax.ShapeDtypeStruct((1, 4, R, COLS), F32),
            jax.ShapeDtypeStruct((1, 4, R, COLS), F32),
            jax.ShapeDtypeStruct((1, 4, COLS), F32),
        ),
        in_specs=[pl.BlockSpec(memory_space=pltpu.SMEM)] + [hbm] * 6,
        out_specs=(vmem, vmem, vmem),
        scratch_shapes=[
            pltpu.VMEM((L, D, COLS), BF16),
            pltpu.VMEM((4, R, COLS), BF16),
            pltpu.VMEM((4, R, COLS), BF16),
            pltpu.VMEM((4, COLS), F32),
            pltpu.VMEM((4, 2 * R, COLS), BF16),
            pltpu.VMEM((4, 8, COLS), F32),
            pltpu.VMEM((4, 2 * R, COLS), BF16),
            pltpu.VMEM((4, 8, COLS), F32),
            pltpu.VMEM((2, CHIPS, L * R, COLS), BF16),
            pltpu.VMEM((L, NH, 2, CHIPS, H, COLS), BF16),
            pltpu.VMEM((TOK, COLS), BF16),
            pltpu.VMEM((TOK, COLS), BF16),
            pltpu.VMEM((L, TOK, COLS), F32),
            pltpu.VMEM((L, TOK, R), BF16),
            pltpu.VMEM((L, TOK, COLS), F32),
            pltpu.VMEM((L, 8, COLS), F32),
            pltpu.VMEM((L, 8, COLS), F32),
            pltpu.VMEM((L, NH, CHIPS, H, COLS), BF16),
            pltpu.VMEM((L, NH, CHIPS, H, COLS), BF16),
            pltpu.VMEM((L, NH, EXT, COLS), F32),
            pltpu.VMEM((L, NH, EXT, COLS), F32),
            pltpu.VMEM((L, NH, CHIPS, RSB, COLS), BF16),
            pltpu.VMEM((L, NH, CHIPS, RSB, COLS), BF16),
            pltpu.VMEM((NH, H, COLS), F32),
            pltpu.VMEM((NH, EXT, COLS), F32),
            pltpu.VMEM((R + 8, TOK), F32),
            pltpu.VMEM((R + 8, TOK), F32),
            pltpu.VMEM((R + 8, TOK), F32),
            pltpu.VMEM((CHIPS, R + 8, TOK), F32),
            pltpu.VMEM((L, 2 * R + 8, COLS), F32),
            pltpu.VMEM((L, 2 * R + 8, COLS), F32),
            pltpu.VMEM((L, 2 * R + 8, COLS), F32),
            dma((6,)),
            dma((2, 2)),
            dma((L, 2, WCH)),
            dma((4,)),
            dma((4,)),
            dma((4,)),
            dma((4,)),
            dma,
            dma((3,)),
            dma,
            dma,
            dma((L, NH)),
            dma((L, NH, 3)),
            dma((L, NH, 4)),
            dma((L, NH, 4)),
            dma((L, NH, 4)),
            dma((L, NH, 4)),
            dma((L, NH)),
            dma((L, NH)),
            dma((L, NH)),
            dma((L, NH, 3)),
            dma,
            dma,
            dma,
            dma,
            dma((4,)),
            dma((4,)),
        ],
        compiler_params=pltpu.CompilerParams(
            collective_id=0, has_side_effects=True, vmem_limit_bytes=60 * 2**20
        ),
    )(tenants, inputs, grad_out, base_weight, adapter_a, adapter_b, magnitude)


def solution(mesh):
    return jax.shard_map(
        local,
        mesh=mesh,
        in_specs=(
            P(None, None, "tensor"),
            P(None, None, "tensor"),
            P(),
            P("section", None, "tensor"),
            P("section", None, None, None),
            P("section", None, None, "tensor"),
            P("section", None, "tensor"),
        ),
        out_specs=(
            P("section", None, None, "tensor"),
            P("section", None, None, "tensor"),
            P("section", None, "tensor"),
        ),
        check_vma=False,
    )
```

```python
import jax
import jax.numpy as jnp
from jax import lax
from jax.experimental import pallas as pl
from jax.experimental.pallas import tpu as pltpu
from jax.sharding import PartitionSpec as P

MESH = pl.DeviceIdType.MESH
F32 = jnp.float32
BF16 = jnp.bfloat16
HIGHEST = lax.Precision.HIGHEST

L = 4
TOK = 128
NH = 2
H = TOK // NH
D = 4096
R = 16
COLS = 128
CHIPS = 16
RSB = [H] * (NH - 1) + [H + R]
WCH = 16
WROWS = D // WCH

ROUTES = {
    0: {
        0: [(0, 0, 0, 12), (1, 0, 12, 4), (1, 0, 8, 4), (1, 0, 4, 4), (1, 1, 12, 4), (1, 1, 8, 4)],
        1: [(1, 1, 6, 2), (0, 3, 0, 16)],
        2: [(1, 2, 12, 4)],
    },
    1: {
        0: [
            (1, 1, 12, 4), (1, 1, 8, 4), (1, 1, 6, 2), (1, 1, 0, 6),
            (0, 0, 0, 8), (0, 1, 0, 12), (1, 2, 12, 4), (1, 2, 8, 4),
        ],
        2: [(0, 3, 0, 8)],
    },
    2: {
        0: [
            (0, 2, 0, 8), (1, 2, 12, 4), (1, 2, 8, 4),
            (0, 0, 0, 4), (1, 0, 12, 4), (0, 1, 0, 6), (1, 2, 0, 8),
        ],
        1: [(0, 2, 8, 4)],
    },
    3: {
        0: [(0, 3, 0, 16), (1, 0, 12, 4), (1, 0, 8, 4), (0, 2, 0, 8), (1, 1, 12, 4)],
        1: [(1, 3, 8, 8)],
    },
}


def sent(section, way):
    return sum(e[3] for stage in ROUTES[section].values() for e in stage if e[0] == way)


def awaited(section, layer, stage):
    done = set()
    for k in range(stage + 1):
        for event in ROUTES[section].get(k, []):
            if event[1] == layer:
                done |= set(range(event[2], event[2] + event[3]))
    left = [j for j in range(WCH) if j not in done]
    runs = []
    for j in left:
        if runs and runs[-1][0] + runs[-1][1] == j:
            runs[-1][1] += 1
        else:
            runs.append([j, 1])
    return runs


def hops(r):
    dz, dy = divmod(r, 4)
    return min(dz, 4 - dz) + min(dy, 4 - dy)


NEAR = sorted(range(CHIPS), key=hops)
GROUPS = [(1, 4), (5, 6), (11, 5)]
QUADS = [12, 8, 4, 0]


def inverse(p):
    dz, dy = divmod(NEAR[p], 4)
    return NEAR.index(((4 - dz) % 4) * 4 + (4 - dy) % 4)


def dot(a, b, ca, cb, precision=None):
    return lax.dot_general(
        a, b, (((ca,), (cb,)), ((), ())), precision=precision, preferred_element_type=F32
    )


def split3(v):
    hi = v.astype(BF16)
    rest = v - hi.astype(F32)
    mid = rest.astype(BF16)
    low = (rest - mid.astype(F32)).astype(BF16)
    return jnp.concatenate([hi, mid, low], axis=0)


def fold3(v):
    return v[0:R] + v[R : 2 * R] + v[2 * R : 3 * R]


def kernel(
    ten_ref, x_hbm, g_hbm, w_hbm, a_hbm, b_hbm, m_hbm,
    oa_ref, ob_ref, om_ref,
    w_buf, a_own, b_own, m_own, sm_src, mg_src, sm_buf, mg_buf, ag_a, xg, cur, grad,
    sv_branch, sv_low, sv_root, sv_norm, sv_scale, sv_gb,
    mine_buf, cs_src, cs_dst, ce_src, ce_dst, rs_src, rs_dst, own_sum, own_ext, rank_buf, lx_src, lx_dst, ex_src, ex_dst,
    res, od_src, od_dst,
    loc_sem, w_send, w_recv, sm_send, sm_recv, mg_send, mg_recv,
    aa_send, aa_recv, ac_send, ac_recv,
    ag_send, ag_recv, cf_send, cf_recv,
    cs_send, cs_recv, ce_send, ce_recv, rs_send, rs_recv,
    lx_send, lx_recv, ex_send, ex_recv, od_send, od_recv,
):
    s = lax.axis_index("section")
    t = lax.axis_index("tensor")
    z = t // 8
    y = (t // 2) % 4
    c = t % 2

    def plane(p):
        dz, dy = divmod(NEAR[p], 4)
        return (s, ((z + dz) % 4) * 8 + ((y + dy) % 4) * 2 + c)

    def source(p):
        dz, dy = divmod(NEAR[p], 4)
        return ((z + 4 - dz) % 4) * 4 + (y + 4 - dy) % 4

    partner = (s, t + 1 - 2 * c)

    def section(d):
        return ((s + d) % 4, t)

    def remote(src, dst, send, recv, device):
        return pltpu.make_async_remote_copy(
            src_ref=src, dst_ref=dst, send_sem=send, recv_sem=recv,
            device_id=device, device_id_type=MESH,
        )

    def every(n, fn):
        lax.fori_loop(0, n, lambda i, _: (fn(i), 0)[1], 0)

    def w_copy(way, layer, j, own):
        rows = pl.ds(j * WROWS, WROWS)
        src = w_hbm.at[0, rows] if own else w_buf.at[layer, rows]
        return remote(
            src, w_buf.at[layer, rows], w_send.at[way], w_recv.at[layer, j], section(1 + 2 * way)
        )

    def w_left(way, n):
        while n:
            now = min(n, WCH)
            rows = pl.ds(0, now * WROWS)
            remote(
                w_buf.at[0, rows], w_buf.at[0, rows], w_send.at[way], w_recv.at[0, 0], section(1)
            ).wait_send()
            n -= now

    def sm_copy(d):
        return remote(sm_src.at[d], sm_buf.at[s], sm_send.at[d], sm_recv.at[d], section(d))

    def mg_copy(d):
        return remote(mg_src.at[d], mg_buf.at[s], mg_send.at[d], mg_recv.at[d], section(d))

    def aa_copy(p, g):
        return remote(ag_a.at[c, 0], ag_a.at[c, p], aa_send, aa_recv.at[g], plane(p))

    def aa_all(first, n, g):
        part = ag_a.at[c, pl.ds(first, n)]
        return remote(part, part, aa_send, aa_recv.at[g], partner)

    def ac_copy(core):
        return remote(ag_a.at[core], ag_a.at[core], ac_send, ac_recv, partner)

    def ag_copy(l, h, p, g):
        return remote(
            xg.at[l, h, c, 0], xg.at[l, h, c, p], ag_send.at[l, h], ag_recv.at[l, h, g], plane(p)
        )

    def ag_all(l, h, first, n, g):
        part = xg.at[l, h, c, pl.ds(first, n)]
        return remote(part, part, ag_send.at[l, h], ag_recv.at[l, h, g], partner)

    def cf_copy(l, h, first, n, g, core):
        part = xg.at[l, h, core, pl.ds(first, n)]
        return remote(part, part, cf_send.at[l, h, g], cf_recv.at[l, h, g], partner)

    def cs_copy(l, h, q):
        part = pl.ds(QUADS[q], 4)
        return remote(
            cs_src.at[l, h, part], cs_dst.at[l, h, part],
            cs_send.at[l, h, q], cs_recv.at[l, h, q], partner,
        )

    def ce_copy(l):
        return remote(ce_src.at[l], ce_dst.at[l], ce_send.at[l], ce_recv.at[l], partner)

    def rs_copy(l, h, p, g):
        return remote(
            rs_src.at[l, h, p, pl.ds(0, RSB[h])], rs_dst.at[l, h, p, pl.ds(0, RSB[h])],
            rs_send.at[l, h], rs_recv.at[l, h, g], plane(p),
        )

    def rs_all(l, h, first, n, g):
        part = pl.ds(first, n)
        return remote(
            rs_src.at[l, h, part, pl.ds(0, RSB[h])], rs_dst.at[l, h, part, pl.ds(0, RSB[h])],
            rs_send.at[l, h], rs_recv.at[l, h, g], partner,
        )

    def lx_copy(first, n):
        rows, k = pl.ds(first, n), int(first > 0)
        return remote(lx_src.at[rows], lx_dst.at[rows], lx_send.at[k], lx_recv.at[k], partner)

    def ex_copy(p, first, n):
        rows, k = pl.ds(first, n), int(first > 0)
        return remote(
            ex_src.at[rows], ex_dst.at[p, rows], ex_send.at[k], ex_recv.at[k], plane(p)
        )

    def ex_all(first, n):
        part, k = ex_dst.at[pl.ds(1, CHIPS - 1), pl.ds(first, n)], int(first > 0)
        return remote(part, part, ex_send.at[k], ex_recv.at[k], partner)

    def od_copy(d):
        return remote(
            od_src.at[(s + d) % 4], od_dst.at[s], od_send.at[d], od_recv.at[d], section(d)
        )

    def group_of(p):
        return [g for g, (first, n) in enumerate(GROUPS) if first <= p < first + n][0]

    barrier = pltpu.get_barrier_semaphore()
    peers = [plane(p) for p in reversed(range(1, CHIPS))]
    peers += [section(d) for d in (2, 1, 3)] + [partner]
    for peer in peers:
        pl.semaphore_signal(barrier, inc=1, device_id=peer, device_id_type=MESH)

    own_x = pltpu.make_async_copy(x_hbm.at[s], cur, loc_sem.at[0])
    own_x.start()
    own_a = pltpu.make_async_copy(
        a_hbm.at[0, :, :, pl.ds(pl.multiple_of(t * COLS, COLS), COLS)], a_own, loc_sem.at[1]
    )
    own_a.start()
    own_b = pltpu.make_async_copy(b_hbm.at[0], b_own, loc_sem.at[2])
    own_b.start()
    own_m = pltpu.make_async_copy(m_hbm.at[0], m_own, loc_sem.at[3])
    own_m.start()
    own_w = pltpu.make_async_copy(w_hbm.at[0], w_buf.at[s], loc_sem.at[4])
    own_w.start()
    own_g = pltpu.make_async_copy(g_hbm.at[s], grad, loc_sem.at[5])
    own_g.start()

    own_a.wait()
    own_b.wait()
    own_m.wait()
    for d in range(4):
        tenant = ten_ref[(s + d) % 4]
        pair = jnp.concatenate([a_own[tenant], b_own[tenant]], axis=0)
        mag = jnp.broadcast_to(m_own[pl.ds(tenant, 1), :], (8, COLS))
        if d == 0:
            sm_buf[s] = pair
            mg_buf[s] = mag
        else:
            sm_src[d] = pair
            mg_src[d] = mag
    own_x.wait()

    pl.semaphore_wait(barrier, len(peers))

    for d in (2, 1, 3):
        sm_copy(d).start()
        mg_copy(d).start()

    def send_block(l, h):
        xg[l, h, c, 0] = cur[h * H : (h + 1) * H]
        for p in reversed(range(1, CHIPS)):
            ag_copy(l, h, p, group_of(p)).start()
        cf_copy(l, h, 0, 1, 3, c).start()

    def split_stage(k):
        events = ROUTES[k][0]
        n = 0
        while n < len(events) and events[n][1] == k:
            n += 1
        return events[:n], events[n:]

    def send_events(k, events):
        for way, layer, first, n in events:

            def one(j):
                copy = w_copy(way, layer, first + j, layer == k)
                if layer != k:
                    copy.wait_recv()
                copy.start()

            every(n, one)

    def in_section(fn):
        for k in range(4):

            @pl.when(s == k)
            def _():
                fn(k)

    in_section(lambda k: send_events(k, split_stage(k)[0]))

    for h in range(NH):
        send_block(0, h)
    for d in range(1, 4):
        sm_copy(d).wait_recv()
        mg_copy(d).wait_recv()
    for l in range(L):
        ag_a[c, 0, l * R : (l + 1) * R] = sm_buf[l, 0:R]
    for p in reversed(range(1, CHIPS)):
        aa_copy(p, group_of(p)).start()

    in_section(lambda k: send_events(k, split_stage(k)[1]))
    own_w.wait()
    own_g.wait()

    for g, (first, n) in enumerate(GROUPS):
        aa_all(first, n, g).wait_recv()
    ac_copy(c).start()
    ac_copy(1 - c).wait_recv()

    def weights_of(k, l):
        if l:
            send_events(k, ROUTES[k].get(l, []))
        if l != k:
            for first, n in awaited(k, l, l):
                every(n, lambda j: w_copy(0, l, first + j, False).wait_recv())

    def a_rows(l, p):
        rows = pl.ds(pl.multiple_of(l * R, R), R)
        return jnp.concatenate([ag_a[0, p, rows, :], ag_a[1, p, rows, :]], axis=1)

    def local_grads(l):
        up = grad[...].astype(F32)
        gm = jnp.sum(up * sv_branch[l], axis=0, keepdims=True) / sv_norm[l, 0:1]
        res[l, R : 2 * R] = dot(sv_low[l], sv_gb[...], 0, 0)
        res[l, 2 * R : 2 * R + 8] = jnp.broadcast_to(gm, (8, COLS))

    def begin(l, h):
        tokens = slice(h * H, (h + 1) * H)
        branch = sv_branch[l, tokens]
        b_l = sm_buf[l, R : 2 * R]
        grad_branch = (grad[tokens].astype(F32) * sv_scale[l, 0:1]).astype(BF16)
        sv_gb[tokens] = grad_branch
        last = h == NH - 1
        if last:
            ce_src[l] = dot(b_l, sv_gb[...], 1, 1)
            ce_copy(l).start()
        rank = dot(grad_branch, b_l, 1, 1)
        rank_hi = rank.astype(BF16)
        rank_lo = (rank - rank_hi.astype(F32)).astype(BF16)
        rank_two = jnp.concatenate([rank_hi, rank_lo], axis=1)
        row = jnp.sum(grad_branch.astype(F32) * branch, axis=1, keepdims=True)
        share = row * (1.0 / D) / sv_root[l, tokens]

        def part(p):
            q = inverse(p)
            rows = w_buf[l, pl.ds(pl.multiple_of(source(q) * 256, 256), 256), :]
            a_q = a_rows(l, q)
            both = dot(grad_branch, rows, 1, 1) + dot(
                rank_two, jnp.concatenate([a_q, a_q], axis=0), 1, 0
            )
            zero = both[:, 0:COLS] - xg[l, h, 0, q].astype(F32) * share
            one = both[:, COLS:] - xg[l, h, 1, q].astype(F32) * share
            return jnp.where(c == 0, one, zero), jnp.where(c == 0, zero, one)

        def work(q):
            for p in range(QUADS[q], QUADS[q] + 4):
                theirs, mine = part(p)
                cs_src[l, h, p] = theirs.astype(BF16)
                mine_buf[p] = mine
            cs_copy(l, h, q).start()

        work(0)
        work(1)
        for q in range(4):
            if q < 2:
                work(q + 2)
            if last and q == 0:
                ce_copy(l).wait_recv()
                ext = ce_src[l] + ce_dst[l]
                own_ext[...] = ext
                ext_b = ext.astype(BF16)
            cs_copy(l, h, q).wait_recv()
            for p in reversed(range(QUADS[q], QUADS[q] + 4)):
                total = mine_buf[p] + cs_dst[l, h, p].astype(F32)
                if p:
                    rs_src[l, h, p, 0:H] = total.astype(BF16)
                    if last:
                        rs_src[l, h, p, H : H + R] = ext_b
                    rs_copy(l, h, p, group_of(p)).start()
                else:
                    own_sum[h] = total
        if last:
            local_grads(l)

    def normed_own(l):
        x_own = jnp.concatenate([xg[l, i, c, 0] for i in range(NH)], axis=0)
        return (x_own.astype(F32) / sv_root[l]).astype(BF16)

    def adapter_grad(l, rank_sum):
        res[l, 0:R] = fold3(dot(split3(rank_sum), normed_own(l), 1, 0))

    def finish(l, h):
        tokens = slice(h * H, (h + 1) * H)
        total = own_sum[h]
        rank_sum = own_ext[...]
        for g, (first, n) in enumerate(GROUPS):
            rs_all(l, h, first, n, g).wait_recv()
            for p in range(first, first + n):
                total = total + rs_dst[l, h, p, 0:H].astype(F32)
                if h == NH - 1:
                    rank_sum = rank_sum + rs_dst[l, h, p, H : H + R].astype(F32)
        state = grad[tokens].astype(F32) + total / sv_root[l, tokens]
        grad[tokens] = state.astype(BF16)
        return rank_sum

    def w_rows(l, p):
        return w_buf[l, pl.ds(pl.multiple_of(source(p) * 256, 256), 256), :]

    def column_norms(l):
        def squares(i, total):
            rows = w_buf[l, pl.ds(pl.multiple_of(i * 256, 256), 256), :].astype(F32)
            return total + jnp.sum((rows * rows).reshape(32, 8, COLS), axis=0)

        base_sq = jnp.sum(
            lax.fori_loop(0, 16, squares, jnp.zeros((8, COLS), F32)), axis=0, keepdims=True
        )
        cross = jnp.zeros((R, COLS), F32)
        gram = jnp.zeros((R, R), F32)
        for p in range(CHIPS):
            a_p = a_rows(l, p)
            cross = cross + dot(a_p, w_rows(l, p), 1, 0)
            gram = gram + dot(a_p, a_p, 1, 1)
        b_wide = sm_buf[l, R : 2 * R].astype(F32)
        quad = dot(gram, b_wide, 1, 0, HIGHEST)
        total = base_sq + jnp.sum(b_wide * (2.0 * cross + quad), axis=0, keepdims=True)
        norm = jnp.sqrt(total + 1e-06)
        sv_norm[l] = jnp.broadcast_to(norm, (8, COLS))
        sv_scale[l] = jnp.broadcast_to(mg_buf[l, 0:1] / norm, (8, COLS))

    def forward(l, _):
        for layer in range(L):

            @pl.when(l == layer)
            def _():
                in_section(lambda k: weights_of(k, layer))

        column_norms(l)
        for h in range(NH):
            tokens = slice(h * H, (h + 1) * H)
            acc = jnp.zeros((H, COLS), F32)
            low_acc = jnp.zeros((H, R), F32)
            ssq = jnp.zeros((H, COLS), F32)

            def use(first, n, g, acc, low_acc, ssq):
                cf_copy(l, h, first, n, g, 1 - c).wait_recv()
                for p in range(first, first + n):
                    both = jnp.concatenate([xg[l, h, 0, p], xg[l, h, 1, p]], axis=1)
                    acc = acc + dot(both, w_rows(l, p), 1, 0)
                    low_acc = low_acc + dot(both, a_rows(l, p), 1, 1)
                    wide = both.astype(F32)
                    wide = wide * wide
                    ssq = ssq + wide[:, 0:COLS] + wide[:, COLS:]
                return acc, low_acc, ssq

            before = (0, 1, 3)
            for g, (first, n) in enumerate(GROUPS):
                ag_all(l, h, first, n, g).wait_recv()
                cf_copy(l, h, first, n, g, c).start()
                acc, low_acc, ssq = use(*before, acc, low_acc, ssq)
                before = (first, n, g)
            acc, low_acc, ssq = use(*before, acc, low_acc, ssq)

            mean = jnp.sum(ssq, axis=1, keepdims=True) * (1.0 / D)
            root = jnp.sqrt(mean + 1e-05)
            inv = 1.0 / root
            low = (low_acc * inv).astype(BF16)
            branch = acc * inv + dot(low, sm_buf[l, R : 2 * R], 1, 0)
            sv_branch[l, tokens] = branch
            sv_low[l, tokens] = low
            sv_root[l, tokens] = jnp.broadcast_to(root, (H, COLS))
            state = cur[tokens].astype(F32) + sv_scale[l, 0:1] * branch
            cur[tokens] = state.astype(BF16)

            @pl.when(l < L - 1)
            def _():
                send_block(l + 1, h)

            @pl.when(l == L - 1)
            def _():
                begin(L - 1, h)

        return 0

    lax.fori_loop(0, L, forward, 0)

    def backward(i, _):
        l = L - 1 - i
        for h in range(NH):
            rank_sum = finish(l, h)
            if h == NH - 1:
                rank_buf[...] = rank_sum

            @pl.when(l > 1)
            def _():
                begin(l - 1, h)

        @pl.when(l > 1)
        def _():
            adapter_grad(l, rank_buf[...])

        return 0

    lax.fori_loop(0, L - 1, backward, 0)

    sv_gb[...] = (grad[...].astype(F32) * sv_scale[0, 0:1]).astype(BF16)
    lx_src[0:R] = dot(sm_buf[0, R : 2 * R], sv_gb[...], 1, 1)
    lx_copy(0, R).start()
    adapter_grad(1, rank_buf[...])
    local_grads(0)
    sum_a = jnp.zeros((1, COLS), F32)
    sum_b = jnp.zeros((1, COLS), F32)
    sum_m = jnp.zeros((1, COLS), F32)
    for l in range(L):
        if l:
            ga = res[l, 0:R]
            sum_a = sum_a + jnp.sum(ga * ga, axis=0, keepdims=True)
        gb = res[l, R : 2 * R]
        sum_b = sum_b + jnp.sum(gb * gb, axis=0, keepdims=True)
        gm = res[l, 2 * R : 2 * R + 1]
        sum_m = sum_m + gm * gm
    lx_src[R : R + 8] = jnp.concatenate([sum_a, sum_b, sum_m, jnp.zeros((5, COLS), F32)], axis=0)
    lx_copy(R, 8).start()
    lx_copy(0, R).wait_recv()
    rank_sum = lx_src[0:R] + lx_dst[0:R]
    ex_src[0:R] = rank_sum
    for p in reversed(range(1, CHIPS)):
        ex_copy(p, 0, R).start()
    lx_copy(R, 8).wait_recv()
    sums = lx_src[R : R + 8] + lx_dst[R : R + 8]
    ex_src[R : R + 8] = sums
    for p in reversed(range(1, CHIPS)):
        ex_copy(p, R, 8).start()
    normed = normed_own(0)
    outer = jnp.zeros((TOK, TOK), F32)
    for p in range(CHIPS):
        both = jnp.concatenate(
            [
                jnp.concatenate([xg[0, h, 0, p], xg[0, h, 1, p]], axis=1)
                for h in range(NH)
            ],
            axis=0,
        )
        outer = outer + dot(both, both, 1, 1)
    inv = 1.0 / sv_root[0]
    outer = outer * inv * inv.T
    outer_hi = outer.astype(BF16)
    outer_lo = (outer - outer_hi.astype(F32)).astype(BF16)
    right = jnp.concatenate([normed, outer_hi, outer_lo], axis=1)
    ex_all(R, 8).wait_recv()
    for p in range(1, CHIPS):
        sums = sums + ex_dst[p, R : R + 8]
    ex_all(0, R).wait_recv()
    for p in range(1, CHIPS):
        rank_sum = rank_sum + ex_dst[p, 0:R]
    made = fold3(dot(split3(rank_sum), right, 1, 0))
    res[0, 0:R] = made[:, 0:COLS]
    sq = rank_sum * (made[:, COLS : 2 * COLS] + made[:, 2 * COLS :])

    def norm_of(v, count):
        return 1.0 / jnp.sqrt(jnp.sum(v, axis=1, keepdims=True) * (1.0 / count) + 1e-06)

    by_a = norm_of(sums[0:1] + jnp.sum(sq, axis=0, keepdims=True), L * R * D)
    by_b = norm_of(sums[1:2], L * R * D)
    by_m = norm_of(sums[2:3], L * D)
    for l in range(L):
        od_src[l, 0:R] = res[l, 0:R] * by_a
        od_src[l, R : 2 * R] = res[l, R : 2 * R] * by_b
        od_src[l, 2 * R : 2 * R + 8] = res[l, 2 * R : 2 * R + 8] * by_m
    for d in (2, 1, 3):
        od_copy(d).start()
    od_dst[s] = od_src[s]

    def drain_w(k):
        for way in range(2):
            w_left(way, sent(k, way))

    in_section(drain_w)
    aa_all(1, CHIPS - 1, 0).wait_send()
    ac_copy(c).wait_send()

    def drain_l(l):
        for h in range(NH):
            ag_all(l, h, 1, CHIPS - 1, 0).wait_send()
            cf_copy(l, h, 0, 1, 3, c).wait_send()
            for g, (first, n) in enumerate(GROUPS):
                cf_copy(l, h, first, n, g, c).wait_send()

    every(L, drain_l)

    def drain_b(i):
        l = i + 1
        for h in range(NH):
            rs_all(l, h, 1, CHIPS - 1, 0).wait_send()
            for q in range(4):
                cs_copy(l, h, q).wait_send()
        ce_copy(l).wait_send()

    every(L - 1, drain_b)
    lx_copy(0, R).wait_send()
    lx_copy(R, 8).wait_send()
    ex_all(0, R).wait_send()
    ex_all(R, 8).wait_send()
    for d in range(1, 4):
        sm_copy(d).wait_send()
        mg_copy(d).wait_send()

    for d in (1, 3, 2):
        od_copy(d).wait_recv()
    for tenant in range(4):
        out = jnp.zeros((2 * R + 8, COLS), F32)
        for k in range(4):
            out = jnp.where(ten_ref[k] == tenant, od_dst[k], out)
        oa_ref[0, tenant] = out[0:R]
        ob_ref[0, tenant] = out[R : 2 * R]
        om_ref[0, pl.ds(tenant, 1), :] = out[2 * R : 2 * R + 1]
    for d in range(1, 4):
        od_copy(d).wait_send()


def local(inputs, grad_out, tenants, base_weight, adapter_a, adapter_b, magnitude):
    vmem = pl.BlockSpec(memory_space=pltpu.VMEM)
    hbm = pl.BlockSpec(memory_space=pl.ANY)
    dma = pltpu.SemaphoreType.DMA
    return pl.pallas_call(
        kernel,
        out_shape=(
            jax.ShapeDtypeStruct((1, 4, R, COLS), F32),
            jax.ShapeDtypeStruct((1, 4, R, COLS), F32),
            jax.ShapeDtypeStruct((1, 4, COLS), F32),
        ),
        in_specs=[pl.BlockSpec(memory_space=pltpu.SMEM)] + [hbm] * 6,
        out_specs=(vmem, vmem, vmem),
        scratch_shapes=[
            pltpu.VMEM((L, D, COLS), BF16),
            pltpu.VMEM((4, R, COLS), BF16),
            pltpu.VMEM((4, R, COLS), BF16),
            pltpu.VMEM((4, COLS), F32),
            pltpu.VMEM((4, 2 * R, COLS), BF16),
            pltpu.VMEM((4, 8, COLS), F32),
            pltpu.VMEM((4, 2 * R, COLS), BF16),
            pltpu.VMEM((4, 8, COLS), F32),
            pltpu.VMEM((2, CHIPS, L * R, COLS), BF16),
            pltpu.VMEM((L, NH, 2, CHIPS, H, COLS), BF16),
            pltpu.VMEM((TOK, COLS), BF16),
            pltpu.VMEM((TOK, COLS), BF16),
            pltpu.VMEM((L, TOK, COLS), F32),
            pltpu.VMEM((L, TOK, R), BF16),
            pltpu.VMEM((L, TOK, COLS), F32),
            pltpu.VMEM((L, 8, COLS), F32),
            pltpu.VMEM((L, 8, COLS), F32),
            pltpu.VMEM((TOK, COLS), BF16),
            pltpu.VMEM((CHIPS, H, COLS), F32),
            pltpu.VMEM((L, NH, CHIPS, H, COLS), BF16),
            pltpu.VMEM((L, NH, CHIPS, H, COLS), BF16),
            pltpu.VMEM((L, R, TOK), F32),
            pltpu.VMEM((L, R, TOK), F32),
            pltpu.VMEM((L, NH, CHIPS, H + R, COLS), BF16),
            pltpu.VMEM((L, NH, CHIPS, H + R, COLS), BF16),
            pltpu.VMEM((NH, H, COLS), F32),
            pltpu.VMEM((R, TOK), F32),
            pltpu.VMEM((R, TOK), F32),
            pltpu.VMEM((R + 8, TOK), F32),
            pltpu.VMEM((R + 8, TOK), F32),
            pltpu.VMEM((R + 8, TOK), F32),
            pltpu.VMEM((CHIPS, R + 8, TOK), F32),
            pltpu.VMEM((L, 2 * R + 8, COLS), F32),
            pltpu.VMEM((L, 2 * R + 8, COLS), F32),
            pltpu.VMEM((L, 2 * R + 8, COLS), F32),
            dma((6,)),
            dma((2,)),
            dma((L, WCH)),
            dma((4,)),
            dma((4,)),
            dma((4,)),
            dma((4,)),
            dma,
            dma((3,)),
            dma,
            dma,
            dma((L, NH)),
            dma((L, NH, 3)),
            dma((L, NH, 4)),
            dma((L, NH, 4)),
            dma((L, NH, 4)),
            dma((L, NH, 4)),
            dma((L,)),
            dma((L,)),
            dma((L, NH)),
            dma((L, NH, 3)),
            dma((2,)),
            dma((2,)),
            dma((2,)),
            dma((2,)),
            dma((4,)),
            dma((4,)),
        ],
        compiler_params=pltpu.CompilerParams(
            collective_id=0, has_side_effects=True, vmem_limit_bytes=60 * 2**20
        ),
    )(tenants, inputs, grad_out, base_weight, adapter_a, adapter_b, magnitude)


def solution(mesh):
    return jax.shard_map(
        local,
        mesh=mesh,
        in_specs=(
            P(None, None, "tensor"),
            P(None, None, "tensor"),
            P(),
            P("section", None, "tensor"),
            P("section", None, None, None),
            P("section", None, None, "tensor"),
            P("section", None, "tensor"),
        ),
        out_specs=(
            P("section", None, None, "tensor"),
            P("section", None, None, "tensor"),
            P("section", None, "tensor"),
        ),
        check_vma=False,
    )
```

```python
import jax
import jax.numpy as jnp
from jax import lax
from jax.experimental import pallas as pl
from jax.experimental.pallas import tpu as pltpu
from jax.sharding import PartitionSpec as P

MESH = pl.DeviceIdType.MESH
F32 = jnp.float32
BF16 = jnp.bfloat16
HIGHEST = lax.Precision.HIGHEST

L = 4
TOK = 128
NH = 2
H = TOK // NH
D = 4096
R = 16
COLS = 128
CHIPS = 16
RSB = [H] * (NH - 1) + [H + R]
WCH = 16
WROWS = D // WCH

ROUTES = {
    0: {
        0: [(0, 0, 0, 12), (1, 0, 12, 4), (1, 0, 8, 4), (1, 0, 4, 4), (1, 1, 12, 4), (1, 1, 8, 4)],
        1: [(1, 1, 6, 2), (0, 3, 0, 16)],
        2: [(1, 2, 12, 4)],
    },
    1: {
        0: [
            (1, 1, 12, 4), (1, 1, 8, 4), (1, 1, 6, 2), (1, 1, 0, 6),
            (0, 0, 0, 8), (0, 1, 0, 12), (1, 2, 12, 4), (1, 2, 8, 4),
        ],
        2: [(0, 3, 0, 8)],
    },
    2: {
        0: [
            (0, 2, 0, 8), (1, 2, 12, 4), (1, 2, 8, 4),
            (0, 0, 0, 4), (1, 0, 12, 4), (0, 1, 0, 6), (1, 2, 0, 8),
        ],
        1: [(0, 2, 8, 4)],
    },
    3: {
        0: [(0, 3, 0, 16), (1, 0, 12, 4), (1, 0, 8, 4), (0, 2, 0, 8), (1, 1, 12, 4)],
        1: [(1, 3, 8, 8)],
    },
}


def sent(section, way):
    return sum(e[3] for stage in ROUTES[section].values() for e in stage if e[0] == way)


def awaited(section, layer, stage):
    done = set()
    for k in range(stage + 1):
        for event in ROUTES[section].get(k, []):
            if event[1] == layer:
                done |= set(range(event[2], event[2] + event[3]))
    left = [j for j in range(WCH) if j not in done]
    runs = []
    for j in left:
        if runs and runs[-1][0] + runs[-1][1] == j:
            runs[-1][1] += 1
        else:
            runs.append([j, 1])
    return runs


def hops(r):
    dz, dy = divmod(r, 4)
    return min(dz, 4 - dz) + min(dy, 4 - dy)


NEAR = sorted(range(CHIPS), key=hops)
GROUPS = [(1, 4), (5, 11)]
RS_GROUPS = [(1, 4), (5, 11)]
RUNS = [8, 0]


def inverse(p):
    dz, dy = divmod(NEAR[p], 4)
    return NEAR.index(((4 - dz) % 4) * 4 + (4 - dy) % 4)


def dot(a, b, ca, cb, precision=None):
    return lax.dot_general(
        a, b, (((ca,), (cb,)), ((), ())), precision=precision, preferred_element_type=F32
    )


def split3(v):
    hi = v.astype(BF16)
    rest = v - hi.astype(F32)
    mid = rest.astype(BF16)
    low = (rest - mid.astype(F32)).astype(BF16)
    return jnp.concatenate([hi, mid, low], axis=0)


def fold3(v):
    return v[0:R] + v[R : 2 * R] + v[2 * R : 3 * R]


def kernel(
    ten_ref, x_hbm, g_hbm, w_hbm, a_hbm, b_hbm, m_hbm,
    oa_ref, ob_ref, om_ref,
    w_buf, a_own, b_own, m_own, sm_src, mg_src, sm_buf, mg_buf, ag_a, xg, cur, grad,
    sv_branch, sv_low, sv_root, sv_norm, sv_scale, sv_gb,
    mine_buf, cs_src, cs_dst, ce_src, ce_dst, rs_src, rs_dst, own_sum, own_ext, rank_buf, lx_src, lx_dst, ex_src, ex_dst,
    res, od_src, od_dst,
    loc_sem, w_send, w_recv, sm_send, sm_recv, mg_send, mg_recv,
    aa_send, aa_recv, ac_send, ac_recv,
    ag_send, ag_recv, cf_send, cf_recv,
    cs_send, cs_recv, ce_send, ce_recv, rs_send, rs_recv,
    lx_send, lx_recv, ex_send, ex_recv, od_send, od_recv,
):
    s = lax.axis_index("section")
    t = lax.axis_index("tensor")
    z = t // 8
    y = (t // 2) % 4
    c = t % 2

    def plane(p):
        dz, dy = divmod(NEAR[p], 4)
        return (s, ((z + dz) % 4) * 8 + ((y + dy) % 4) * 2 + c)

    def source(p):
        dz, dy = divmod(NEAR[p], 4)
        return ((z + 4 - dz) % 4) * 4 + (y + 4 - dy) % 4

    partner = (s, t + 1 - 2 * c)

    def section(d):
        return ((s + d) % 4, t)

    def remote(src, dst, send, recv, device):
        return pltpu.make_async_remote_copy(
            src_ref=src, dst_ref=dst, send_sem=send, recv_sem=recv,
            device_id=device, device_id_type=MESH,
        )

    def every(n, fn):
        lax.fori_loop(0, n, lambda i, _: (fn(i), 0)[1], 0)

    def w_copy(way, layer, j, own):
        rows = pl.ds(j * WROWS, WROWS)
        src = w_hbm.at[0, rows] if own else w_buf.at[layer, rows]
        return remote(
            src, w_buf.at[layer, rows], w_send.at[way], w_recv.at[layer, j], section(1 + 2 * way)
        )

    def w_left(way, n):
        while n:
            now = min(n, WCH)
            rows = pl.ds(0, now * WROWS)
            remote(
                w_buf.at[0, rows], w_buf.at[0, rows], w_send.at[way], w_recv.at[0, 0], section(1)
            ).wait_send()
            n -= now

    def sm_copy(d):
        return remote(sm_src.at[d], sm_buf.at[s], sm_send.at[d], sm_recv.at[d], section(d))

    def mg_copy(d):
        return remote(mg_src.at[d], mg_buf.at[s], mg_send.at[d], mg_recv.at[d], section(d))

    def aa_copy(p, g):
        return remote(ag_a.at[c, 0], ag_a.at[c, p], aa_send, aa_recv.at[g], plane(p))

    def aa_all(first, n, g):
        part = ag_a.at[c, pl.ds(first, n)]
        return remote(part, part, aa_send, aa_recv.at[g], partner)

    def ac_copy(core):
        return remote(ag_a.at[core], ag_a.at[core], ac_send, ac_recv, partner)

    def ag_copy(l, h, p, g):
        return remote(
            xg.at[l, h, c, 0], xg.at[l, h, c, p], ag_send.at[l, h], ag_recv.at[l, h, g], plane(p)
        )

    def ag_all(l, h, first, n, g):
        part = xg.at[l, h, c, pl.ds(first, n)]
        return remote(part, part, ag_send.at[l, h], ag_recv.at[l, h, g], partner)

    def cf_copy(l, h, first, n, g, core):
        part = xg.at[l, h, core, pl.ds(first, n)]
        return remote(part, part, cf_send.at[l, h, g], cf_recv.at[l, h, g], partner)

    def cs_copy(l, h, q):
        part = pl.ds(RUNS[q], 8)
        return remote(
            cs_src.at[l, h, part], cs_dst.at[l, h, part],
            cs_send.at[l, h, q], cs_recv.at[l, h, q], partner,
        )

    def ce_copy(l):
        return remote(ce_src.at[l], ce_dst.at[l], ce_send.at[l], ce_recv.at[l], partner)

    def rs_copy(l, h, p, g):
        return remote(
            rs_src.at[l, h, p, pl.ds(0, RSB[h])], rs_dst.at[l, h, p, pl.ds(0, RSB[h])],
            rs_send.at[l, h], rs_recv.at[l, h, g], plane(p),
        )

    def rs_all(l, h, first, n, g):
        part = pl.ds(first, n)
        return remote(
            rs_src.at[l, h, part, pl.ds(0, RSB[h])], rs_dst.at[l, h, part, pl.ds(0, RSB[h])],
            rs_send.at[l, h], rs_recv.at[l, h, g], partner,
        )

    def lx_copy(first, n):
        rows, k = pl.ds(first, n), int(first > 0)
        return remote(lx_src.at[rows], lx_dst.at[rows], lx_send.at[k], lx_recv.at[k], partner)

    def ex_copy(p, first, n):
        rows, k = pl.ds(first, n), int(first > 0)
        return remote(
            ex_src.at[rows], ex_dst.at[p, rows], ex_send.at[k], ex_recv.at[k], plane(p)
        )

    def ex_all(first, n):
        part, k = ex_dst.at[pl.ds(1, CHIPS - 1), pl.ds(first, n)], int(first > 0)
        return remote(part, part, ex_send.at[k], ex_recv.at[k], partner)

    def od_copy(d):
        return remote(
            od_src.at[(s + d) % 4], od_dst.at[s], od_send.at[d], od_recv.at[d], section(d)
        )

    def group_of(p, groups=GROUPS):
        return [g for g, (first, n) in enumerate(groups) if first <= p < first + n][0]

    barrier = pltpu.get_barrier_semaphore()
    peers = [plane(p) for p in reversed(range(1, CHIPS))]
    peers += [section(d) for d in (2, 1, 3)] + [partner]
    for peer in peers:
        pl.semaphore_signal(barrier, inc=1, device_id=peer, device_id_type=MESH)

    own_x = pltpu.make_async_copy(x_hbm.at[s], cur, loc_sem.at[0])
    own_x.start()
    own_a = pltpu.make_async_copy(
        a_hbm.at[0, :, :, pl.ds(pl.multiple_of(t * COLS, COLS), COLS)], a_own, loc_sem.at[1]
    )
    own_a.start()
    own_b = pltpu.make_async_copy(b_hbm.at[0], b_own, loc_sem.at[2])
    own_b.start()
    own_m = pltpu.make_async_copy(m_hbm.at[0], m_own, loc_sem.at[3])
    own_m.start()
    own_w = pltpu.make_async_copy(w_hbm.at[0], w_buf.at[s], loc_sem.at[4])
    own_w.start()
    own_g = pltpu.make_async_copy(g_hbm.at[s], grad, loc_sem.at[5])
    own_g.start()

    own_a.wait()
    own_b.wait()
    own_m.wait()
    for d in range(4):
        tenant = ten_ref[(s + d) % 4]
        pair = jnp.concatenate([a_own[tenant], b_own[tenant]], axis=0)
        mag = jnp.broadcast_to(m_own[pl.ds(tenant, 1), :], (8, COLS))
        if d == 0:
            sm_buf[s] = pair
            mg_buf[s] = mag
        else:
            sm_src[d] = pair
            mg_src[d] = mag
    own_x.wait()

    pl.semaphore_wait(barrier, len(peers))

    for d in (2, 1, 3):
        sm_copy(d).start()
        mg_copy(d).start()

    def send_block(l, h):
        xg[l, h, c, 0] = cur[h * H : (h + 1) * H]
        for p in reversed(range(1, CHIPS)):
            ag_copy(l, h, p, group_of(p)).start()
        cf_copy(l, h, 0, 1, 2, c).start()

    def split_stage(k):
        events = ROUTES[k][0]
        n = 0
        while n < len(events) and events[n][1] == k:
            n += 1
        return events[:n], events[n:]

    def send_events(k, events):
        for way, layer, first, n in events:

            def one(j):
                copy = w_copy(way, layer, first + j, layer == k)
                if layer != k:
                    copy.wait_recv()
                copy.start()

            every(n, one)

    def in_section(fn):
        for k in range(4):

            @pl.when(s == k)
            def _():
                fn(k)

    in_section(lambda k: send_events(k, split_stage(k)[0]))

    for h in range(NH):
        send_block(0, h)
    for d in range(1, 4):
        sm_copy(d).wait_recv()
        mg_copy(d).wait_recv()
    for l in range(L):
        ag_a[c, 0, l * R : (l + 1) * R] = sm_buf[l, 0:R]
    for p in reversed(range(1, CHIPS)):
        aa_copy(p, group_of(p)).start()

    in_section(lambda k: send_events(k, split_stage(k)[1]))
    own_w.wait()
    own_g.wait()

    for g, (first, n) in enumerate(GROUPS):
        aa_all(first, n, g).wait_recv()
    ac_copy(c).start()
    ac_copy(1 - c).wait_recv()

    def weights_of(k, l):
        if l:
            send_events(k, ROUTES[k].get(l, []))
        if l != k:
            for first, n in awaited(k, l, l):
                every(n, lambda j: w_copy(0, l, first + j, False).wait_recv())

    def a_rows(l, p):
        rows = pl.ds(pl.multiple_of(l * R, R), R)
        return jnp.concatenate([ag_a[0, p, rows, :], ag_a[1, p, rows, :]], axis=1)

    def local_grads(l):
        up = grad[...].astype(F32)
        gm = jnp.sum(up * sv_branch[l], axis=0, keepdims=True) / sv_norm[l, 0:1]
        res[l, R : 2 * R] = dot(sv_low[l], sv_gb[...], 0, 0)
        res[l, 2 * R : 2 * R + 8] = jnp.broadcast_to(gm, (8, COLS))

    def begin(l, h):
        tokens = slice(h * H, (h + 1) * H)
        branch = sv_branch[l, tokens]
        b_l = sm_buf[l, R : 2 * R]
        grad_branch = (grad[tokens].astype(F32) * sv_scale[l, 0:1]).astype(BF16)
        sv_gb[tokens] = grad_branch
        last = h == NH - 1
        if last:
            ce_src[l] = dot(b_l, sv_gb[...], 1, 1)
            ce_copy(l).start()
        rank = dot(grad_branch, b_l, 1, 1)
        rank_hi = rank.astype(BF16)
        rank_lo = (rank - rank_hi.astype(F32)).astype(BF16)
        rank_two = jnp.concatenate([rank_hi, rank_lo], axis=1)
        row = jnp.sum(grad_branch.astype(F32) * branch, axis=1, keepdims=True)
        share = row * (1.0 / D) / sv_root[l, tokens]

        def part(p):
            q = inverse(p)
            rows = w_buf[l, pl.ds(pl.multiple_of(source(q) * 256, 256), 256), :]
            a_q = a_rows(l, q)
            both = dot(grad_branch, rows, 1, 1) + dot(
                rank_two, jnp.concatenate([a_q, a_q], axis=0), 1, 0
            )
            zero = both[:, 0:COLS] - xg[l, h, 0, q].astype(F32) * share
            one = both[:, COLS:] - xg[l, h, 1, q].astype(F32) * share
            return jnp.where(c == 0, one, zero), jnp.where(c == 0, zero, one)

        def work(q):
            for p in range(RUNS[q], RUNS[q] + 8):
                theirs, mine = part(p)
                cs_src[l, h, p] = theirs.astype(BF16)
                mine_buf[p] = mine
            cs_copy(l, h, q).start()

        work(0)
        work(1)
        for q in range(2):
            if last and q == 0:
                ce_copy(l).wait_recv()
                ext = ce_src[l] + ce_dst[l]
                own_ext[...] = ext
                ext_b = ext.astype(BF16)
            cs_copy(l, h, q).wait_recv()
            for p in reversed(range(RUNS[q], RUNS[q] + 8)):
                total = mine_buf[p] + cs_dst[l, h, p].astype(F32)
                if p:
                    rs_src[l, h, p, 0:H] = total.astype(BF16)
                    if last:
                        rs_src[l, h, p, H : H + R] = ext_b
                    rs_copy(l, h, p, group_of(p, RS_GROUPS)).start()
                else:
                    own_sum[h] = total
        if last:
            local_grads(l)

    def normed_own(l):
        x_own = jnp.concatenate([xg[l, i, c, 0] for i in range(NH)], axis=0)
        return (x_own.astype(F32) / sv_root[l]).astype(BF16)

    def adapter_grad(l, rank_sum):
        res[l, 0:R] = fold3(dot(split3(rank_sum), normed_own(l), 1, 0))

    def finish(l, h):
        tokens = slice(h * H, (h + 1) * H)
        total = own_sum[h]
        rank_sum = own_ext[...]
        for g, (first, n) in enumerate(RS_GROUPS):
            rs_all(l, h, first, n, g).wait_recv()
            for p in range(first, first + n):
                total = total + rs_dst[l, h, p, 0:H].astype(F32)
                if h == NH - 1:
                    rank_sum = rank_sum + rs_dst[l, h, p, H : H + R].astype(F32)
        state = grad[tokens].astype(F32) + total / sv_root[l, tokens]
        grad[tokens] = state.astype(BF16)
        return rank_sum

    def w_rows(l, p):
        return w_buf[l, pl.ds(pl.multiple_of(source(p) * 256, 256), 256), :]

    def column_norms(l):
        def squares(i, total):
            rows = w_buf[l, pl.ds(pl.multiple_of(i * 256, 256), 256), :].astype(F32)
            return total + jnp.sum((rows * rows).reshape(32, 8, COLS), axis=0)

        base_sq = jnp.sum(
            lax.fori_loop(0, 16, squares, jnp.zeros((8, COLS), F32)), axis=0, keepdims=True
        )
        cross = jnp.zeros((R, COLS), F32)
        gram = jnp.zeros((R, R), F32)
        for p in range(CHIPS):
            a_p = a_rows(l, p)
            cross = cross + dot(a_p, w_rows(l, p), 1, 0)
            gram = gram + dot(a_p, a_p, 1, 1)
        b_wide = sm_buf[l, R : 2 * R].astype(F32)
        quad = dot(gram, b_wide, 1, 0, HIGHEST)
        total = base_sq + jnp.sum(b_wide * (2.0 * cross + quad), axis=0, keepdims=True)
        norm = jnp.sqrt(total + 1e-06)
        sv_norm[l] = jnp.broadcast_to(norm, (8, COLS))
        sv_scale[l] = jnp.broadcast_to(mg_buf[l, 0:1] / norm, (8, COLS))

    def forward(l, _):
        for layer in range(L):

            @pl.when(l == layer)
            def _():
                in_section(lambda k: weights_of(k, layer))

        column_norms(l)
        for h in range(NH):
            tokens = slice(h * H, (h + 1) * H)
            acc = jnp.zeros((H, COLS), F32)
            low_acc = jnp.zeros((H, R), F32)
            ssq = jnp.zeros((H, COLS), F32)

            def use(first, n, g, acc, low_acc, ssq):
                cf_copy(l, h, first, n, g, 1 - c).wait_recv()
                for p in range(first, first + n):
                    both = jnp.concatenate([xg[l, h, 0, p], xg[l, h, 1, p]], axis=1)
                    acc = acc + dot(both, w_rows(l, p), 1, 0)
                    low_acc = low_acc + dot(both, a_rows(l, p), 1, 1)
                    wide = both.astype(F32)
                    wide = wide * wide
                    ssq = ssq + wide[:, 0:COLS] + wide[:, COLS:]
                return acc, low_acc, ssq

            before = (0, 1, 2)
            for g, (first, n) in enumerate(GROUPS):
                ag_all(l, h, first, n, g).wait_recv()
                cf_copy(l, h, first, n, g, c).start()
                acc, low_acc, ssq = use(*before, acc, low_acc, ssq)
                before = (first, n, g)
            acc, low_acc, ssq = use(*before, acc, low_acc, ssq)

            mean = jnp.sum(ssq, axis=1, keepdims=True) * (1.0 / D)
            root = jnp.sqrt(mean + 1e-05)
            inv = 1.0 / root
            low = (low_acc * inv).astype(BF16)
            branch = acc * inv + dot(low, sm_buf[l, R : 2 * R], 1, 0)
            sv_branch[l, tokens] = branch
            sv_low[l, tokens] = low
            sv_root[l, tokens] = jnp.broadcast_to(root, (H, COLS))
            state = cur[tokens].astype(F32) + sv_scale[l, 0:1] * branch
            cur[tokens] = state.astype(BF16)

            @pl.when(l < L - 1)
            def _():
                send_block(l + 1, h)

            @pl.when(l == L - 1)
            def _():
                begin(L - 1, h)

        return 0

    lax.fori_loop(0, L, forward, 0)

    def backward(i, _):
        l = L - 1 - i
        for h in range(NH):
            rank_sum = finish(l, h)
            if h == NH - 1:
                rank_buf[...] = rank_sum

            @pl.when(l > 1)
            def _():
                begin(l - 1, h)

        @pl.when(l > 1)
        def _():
            adapter_grad(l, rank_buf[...])

        return 0

    lax.fori_loop(0, L - 1, backward, 0)

    sv_gb[...] = (grad[...].astype(F32) * sv_scale[0, 0:1]).astype(BF16)
    lx_src[0:R] = dot(sm_buf[0, R : 2 * R], sv_gb[...], 1, 1)
    lx_copy(0, R).start()
    adapter_grad(1, rank_buf[...])
    local_grads(0)
    sum_a = jnp.zeros((1, COLS), F32)
    sum_b = jnp.zeros((1, COLS), F32)
    sum_m = jnp.zeros((1, COLS), F32)
    for l in range(L):
        if l:
            ga = res[l, 0:R]
            sum_a = sum_a + jnp.sum(ga * ga, axis=0, keepdims=True)
        gb = res[l, R : 2 * R]
        sum_b = sum_b + jnp.sum(gb * gb, axis=0, keepdims=True)
        gm = res[l, 2 * R : 2 * R + 1]
        sum_m = sum_m + gm * gm
    lx_src[R : R + 8] = jnp.concatenate([sum_a, sum_b, sum_m, jnp.zeros((5, COLS), F32)], axis=0)
    lx_copy(R, 8).start()
    lx_copy(0, R).wait_recv()
    rank_sum = lx_src[0:R] + lx_dst[0:R]
    ex_src[0:R] = rank_sum
    for p in reversed(range(1, CHIPS)):
        ex_copy(p, 0, R).start()
    lx_copy(R, 8).wait_recv()
    sums = lx_src[R : R + 8] + lx_dst[R : R + 8]
    ex_src[R : R + 8] = sums
    for p in reversed(range(1, CHIPS)):
        ex_copy(p, R, 8).start()
    normed = normed_own(0)
    outer = jnp.zeros((TOK, TOK), F32)
    for p in range(CHIPS):
        both = jnp.concatenate(
            [
                jnp.concatenate([xg[0, h, 0, p], xg[0, h, 1, p]], axis=1)
                for h in range(NH)
            ],
            axis=0,
        )
        outer = outer + dot(both, both, 1, 1)
    inv = 1.0 / sv_root[0]
    outer = outer * inv * inv.T
    outer_hi = outer.astype(BF16)
    outer_lo = (outer - outer_hi.astype(F32)).astype(BF16)
    right = jnp.concatenate([normed, outer_hi, outer_lo], axis=1)
    ex_all(R, 8).wait_recv()
    for p in range(1, CHIPS):
        sums = sums + ex_dst[p, R : R + 8]
    ex_all(0, R).wait_recv()
    for p in range(1, CHIPS):
        rank_sum = rank_sum + ex_dst[p, 0:R]
    made = fold3(dot(split3(rank_sum), right, 1, 0))
    res[0, 0:R] = made[:, 0:COLS]
    sq = rank_sum * (made[:, COLS : 2 * COLS] + made[:, 2 * COLS :])

    def norm_of(v, count):
        return 1.0 / jnp.sqrt(jnp.sum(v, axis=1, keepdims=True) * (1.0 / count) + 1e-06)

    by_a = norm_of(sums[0:1] + jnp.sum(sq, axis=0, keepdims=True), L * R * D)
    by_b = norm_of(sums[1:2], L * R * D)
    by_m = norm_of(sums[2:3], L * D)
    for l in range(L):
        od_src[l, 0:R] = res[l, 0:R] * by_a
        od_src[l, R : 2 * R] = res[l, R : 2 * R] * by_b
        od_src[l, 2 * R : 2 * R + 8] = res[l, 2 * R : 2 * R + 8] * by_m
    for d in (2, 1, 3):
        od_copy(d).start()
    od_dst[s] = od_src[s]

    def drain_w(k):
        for way in range(2):
            w_left(way, sent(k, way))

    in_section(drain_w)
    aa_all(1, CHIPS - 1, 0).wait_send()
    ac_copy(c).wait_send()

    def drain_l(l):
        for h in range(NH):
            ag_all(l, h, 1, CHIPS - 1, 0).wait_send()
            cf_copy(l, h, 0, 1, 2, c).wait_send()
            for g, (first, n) in enumerate(GROUPS):
                cf_copy(l, h, first, n, g, c).wait_send()

    every(L, drain_l)

    def drain_b(i):
        l = i + 1
        for h in range(NH):
            rs_all(l, h, 1, CHIPS - 1, 0).wait_send()
            for q in range(2):
                cs_copy(l, h, q).wait_send()
        ce_copy(l).wait_send()

    every(L - 1, drain_b)
    lx_copy(0, R).wait_send()
    lx_copy(R, 8).wait_send()
    ex_all(0, R).wait_send()
    ex_all(R, 8).wait_send()
    for d in range(1, 4):
        sm_copy(d).wait_send()
        mg_copy(d).wait_send()

    for d in (1, 3, 2):
        od_copy(d).wait_recv()
    for tenant in range(4):
        out = jnp.zeros((2 * R + 8, COLS), F32)
        for k in range(4):
            out = jnp.where(ten_ref[k] == tenant, od_dst[k], out)
        oa_ref[0, tenant] = out[0:R]
        ob_ref[0, tenant] = out[R : 2 * R]
        om_ref[0, pl.ds(tenant, 1), :] = out[2 * R : 2 * R + 1]
    for d in range(1, 4):
        od_copy(d).wait_send()


def local(inputs, grad_out, tenants, base_weight, adapter_a, adapter_b, magnitude):
    vmem = pl.BlockSpec(memory_space=pltpu.VMEM)
    hbm = pl.BlockSpec(memory_space=pl.ANY)
    dma = pltpu.SemaphoreType.DMA
    return pl.pallas_call(
        kernel,
        out_shape=(
            jax.ShapeDtypeStruct((1, 4, R, COLS), F32),
            jax.ShapeDtypeStruct((1, 4, R, COLS), F32),
            jax.ShapeDtypeStruct((1, 4, COLS), F32),
        ),
        in_specs=[pl.BlockSpec(memory_space=pltpu.SMEM)] + [hbm] * 6,
        out_specs=(vmem, vmem, vmem),
        scratch_shapes=[
            pltpu.VMEM((L, D, COLS), BF16),
            pltpu.VMEM((4, R, COLS), BF16),
            pltpu.VMEM((4, R, COLS), BF16),
            pltpu.VMEM((4, COLS), F32),
            pltpu.VMEM((4, 2 * R, COLS), BF16),
            pltpu.VMEM((4, 8, COLS), F32),
            pltpu.VMEM((4, 2 * R, COLS), BF16),
            pltpu.VMEM((4, 8, COLS), F32),
            pltpu.VMEM((2, CHIPS, L * R, COLS), BF16),
            pltpu.VMEM((L, NH, 2, CHIPS, H, COLS), BF16),
            pltpu.VMEM((TOK, COLS), BF16),
            pltpu.VMEM((TOK, COLS), BF16),
            pltpu.VMEM((L, TOK, COLS), F32),
            pltpu.VMEM((L, TOK, R), BF16),
            pltpu.VMEM((L, TOK, COLS), F32),
            pltpu.VMEM((L, 8, COLS), F32),
            pltpu.VMEM((L, 8, COLS), F32),
            pltpu.VMEM((TOK, COLS), BF16),
            pltpu.VMEM((CHIPS, H, COLS), F32),
            pltpu.VMEM((L, NH, CHIPS, H, COLS), BF16),
            pltpu.VMEM((L, NH, CHIPS, H, COLS), BF16),
            pltpu.VMEM((L, R, TOK), F32),
            pltpu.VMEM((L, R, TOK), F32),
            pltpu.VMEM((L, NH, CHIPS, H + R, COLS), BF16),
            pltpu.VMEM((L, NH, CHIPS, H + R, COLS), BF16),
            pltpu.VMEM((NH, H, COLS), F32),
            pltpu.VMEM((R, TOK), F32),
            pltpu.VMEM((R, TOK), F32),
            pltpu.VMEM((R + 8, TOK), F32),
            pltpu.VMEM((R + 8, TOK), F32),
            pltpu.VMEM((R + 8, TOK), F32),
            pltpu.VMEM((CHIPS, R + 8, TOK), F32),
            pltpu.VMEM((L, 2 * R + 8, COLS), F32),
            pltpu.VMEM((L, 2 * R + 8, COLS), F32),
            pltpu.VMEM((L, 2 * R + 8, COLS), F32),
            dma((6,)),
            dma((2,)),
            dma((L, WCH)),
            dma((4,)),
            dma((4,)),
            dma((4,)),
            dma((4,)),
            dma,
            dma((3,)),
            dma,
            dma,
            dma((L, NH)),
            dma((L, NH, 3)),
            dma((L, NH, 4)),
            dma((L, NH, 4)),
            dma((L, NH, 4)),
            dma((L, NH, 4)),
            dma((L,)),
            dma((L,)),
            dma((L, NH)),
            dma((L, NH, 3)),
            dma((2,)),
            dma((2,)),
            dma((2,)),
            dma((2,)),
            dma((4,)),
            dma((4,)),
        ],
        compiler_params=pltpu.CompilerParams(
            collective_id=0, has_side_effects=True, vmem_limit_bytes=60 * 2**20
        ),
    )(tenants, inputs, grad_out, base_weight, adapter_a, adapter_b, magnitude)


def solution(mesh):
    return jax.shard_map(
        local,
        mesh=mesh,
        in_specs=(
            P(None, None, "tensor"),
            P(None, None, "tensor"),
            P(),
            P("section", None, "tensor"),
            P("section", None, None, None),
            P("section", None, None, "tensor"),
            P("section", None, "tensor"),
        ),
        out_specs=(
            P("section", None, None, "tensor"),
            P("section", None, None, "tensor"),
            P("section", None, "tensor"),
        ),
        check_vma=False,
    )
```

```python
import jax
import jax.numpy as jnp
from jax import lax
from jax.experimental import pallas as pl
from jax.experimental.pallas import tpu as pltpu
from jax.sharding import PartitionSpec as P

MESH = pl.DeviceIdType.MESH
F32 = jnp.float32
BF16 = jnp.bfloat16
HIGHEST = lax.Precision.HIGHEST

L = 4
TOK = 128
NH = 2
H = TOK // NH
D = 4096
R = 16
COLS = 128
CHIPS = 16
RSB = [H] * (NH - 1) + [H + R]
WCH = 16
WROWS = D // WCH

ROUTES = {
    0: {
        0: [(0, 0, 0, 12), (1, 0, 12, 4), (1, 0, 8, 4), (1, 0, 4, 4), (1, 1, 12, 4), (1, 1, 8, 4)],
        1: [(1, 1, 6, 2), (0, 3, 0, 16)],
        2: [(1, 2, 12, 4)],
    },
    1: {
        0: [
            (1, 1, 12, 4), (1, 1, 8, 4), (1, 1, 6, 2), (1, 1, 0, 6),
            (0, 0, 0, 8), (0, 1, 0, 12), (1, 2, 12, 4), (1, 2, 8, 4),
        ],
        2: [(0, 3, 0, 8)],
    },
    2: {
        0: [
            (0, 2, 0, 8), (1, 2, 12, 4), (1, 2, 8, 4),
            (0, 0, 0, 4), (1, 0, 12, 4), (0, 1, 0, 6), (1, 2, 0, 8),
        ],
        1: [(0, 2, 8, 4)],
    },
    3: {
        0: [(0, 3, 0, 16), (1, 0, 12, 4), (1, 0, 8, 4), (0, 2, 0, 8), (1, 1, 12, 4)],
        1: [(1, 3, 8, 8)],
    },
}


def sent(section, way):
    return sum(e[3] for stage in ROUTES[section].values() for e in stage if e[0] == way)


def awaited(section, layer, stage):
    done = set()
    for k in range(stage + 1):
        for event in ROUTES[section].get(k, []):
            if event[1] == layer:
                done |= set(range(event[2], event[2] + event[3]))
    left = [j for j in range(WCH) if j not in done]
    runs = []
    for j in left:
        if runs and runs[-1][0] + runs[-1][1] == j:
            runs[-1][1] += 1
        else:
            runs.append([j, 1])
    return runs


def hops(r):
    dz, dy = divmod(r, 4)
    return min(dz, 4 - dz) + min(dy, 4 - dy)


NEAR = sorted(range(CHIPS), key=hops)
GROUPS = [(1, 4), (5, 11)]
RS_GROUPS = [(1, 4), (5, 11)]
RUNS = [8, 0]


def inverse(p):
    dz, dy = divmod(NEAR[p], 4)
    return NEAR.index(((4 - dz) % 4) * 4 + (4 - dy) % 4)


def dot(a, b, ca, cb, precision=None):
    return lax.dot_general(
        a, b, (((ca,), (cb,)), ((), ())), precision=precision, preferred_element_type=F32
    )


def split3(v):
    hi = v.astype(BF16)
    rest = v - hi.astype(F32)
    mid = rest.astype(BF16)
    low = (rest - mid.astype(F32)).astype(BF16)
    return jnp.concatenate([hi, mid, low], axis=0)


def fold3(v):
    return v[0:R] + v[R : 2 * R] + v[2 * R : 3 * R]


def kernel(
    ten_ref, x_hbm, g_hbm, w_hbm, a_hbm, b_hbm, m_hbm,
    oa_ref, ob_ref, om_ref,
    w_buf, a_own, b_own, m_own, sm_src, mg_src, sm_buf, mg_buf, ag_a, xg, cur, grad,
    sv_branch, sv_low, sv_root, sv_norm, sv_scale, sv_gb,
    mine_buf, cs_src, cs_dst, ce_src, ce_dst, rs_src, rs_dst, own_sum, own_ext, rank_buf, lx_src, lx_dst, ex_src, ex_dst,
    res, od_src, od_dst,
    loc_sem, w_send, w_recv, sm_send, sm_recv, mg_send, mg_recv,
    aa_send, aa_recv, ac_send, ac_recv,
    ag_send, ag_recv, cf_send, cf_recv,
    cs_send, cs_recv, ce_send, ce_recv, rs_send, rs_recv,
    lx_send, lx_recv, ex_send, ex_recv, od_send, od_recv,
):
    s = lax.axis_index("section")
    t = lax.axis_index("tensor")
    z = t // 8
    y = (t // 2) % 4
    c = t % 2

    def plane(p):
        dz, dy = divmod(NEAR[p], 4)
        return (s, ((z + dz) % 4) * 8 + ((y + dy) % 4) * 2 + c)

    def source(p):
        dz, dy = divmod(NEAR[p], 4)
        return ((z + 4 - dz) % 4) * 4 + (y + 4 - dy) % 4

    partner = (s, t + 1 - 2 * c)

    def section(d):
        return ((s + d) % 4, t)

    def remote(src, dst, send, recv, device):
        return pltpu.make_async_remote_copy(
            src_ref=src, dst_ref=dst, send_sem=send, recv_sem=recv,
            device_id=device, device_id_type=MESH,
        )

    def every(n, fn):
        lax.fori_loop(0, n, lambda i, _: (fn(i), 0)[1], 0)

    def w_copy(way, layer, j, own):
        rows = pl.ds(j * WROWS, WROWS)
        src = w_hbm.at[0, rows] if own else w_buf.at[layer, rows]
        return remote(
            src, w_buf.at[layer, rows], w_send.at[way], w_recv.at[layer, j], section(1 + 2 * way)
        )

    def w_left(way, n):
        while n:
            now = min(n, WCH)
            rows = pl.ds(0, now * WROWS)
            remote(
                w_buf.at[0, rows], w_buf.at[0, rows], w_send.at[way], w_recv.at[0, 0], section(1)
            ).wait_send()
            n -= now

    def sm_copy(d):
        return remote(sm_src.at[d], sm_buf.at[s], sm_send.at[d], sm_recv.at[d], section(d))

    def mg_copy(d):
        return remote(mg_src.at[d], mg_buf.at[s], mg_send.at[d], mg_recv.at[d], section(d))

    def aa_copy(p, g):
        return remote(ag_a.at[c, 0], ag_a.at[c, p], aa_send, aa_recv.at[g], plane(p))

    def aa_all(first, n, g):
        part = ag_a.at[c, pl.ds(first, n)]
        return remote(part, part, aa_send, aa_recv.at[g], partner)

    def ac_copy(core):
        return remote(ag_a.at[core], ag_a.at[core], ac_send, ac_recv, partner)

    def ag_copy(l, h, p, g):
        return remote(
            xg.at[l, h, c, 0], xg.at[l, h, c, p], ag_send.at[l, h], ag_recv.at[l, h, g], plane(p)
        )

    def ag_all(l, h, first, n, g):
        part = xg.at[l, h, c, pl.ds(first, n)]
        return remote(part, part, ag_send.at[l, h], ag_recv.at[l, h, g], partner)

    def cf_copy(l, h, first, n, g, core):
        part = xg.at[l, h, core, pl.ds(first, n)]
        return remote(part, part, cf_send.at[l, h, g], cf_recv.at[l, h, g], partner)

    def cs_copy(l, h, q):
        part = pl.ds(RUNS[q], 8)
        return remote(
            cs_src.at[l, h, part], cs_dst.at[l, h, part],
            cs_send.at[l, h, q], cs_recv.at[l, h, q], partner,
        )

    def ce_copy(l):
        return remote(ce_src.at[l], ce_dst.at[l], ce_send.at[l], ce_recv.at[l], partner)

    def rs_copy(l, h, p, g):
        return remote(
            rs_src.at[l, h, p, pl.ds(0, RSB[h])], rs_dst.at[l, h, p, pl.ds(0, RSB[h])],
            rs_send.at[l, h], rs_recv.at[l, h, g], plane(p),
        )

    def rs_all(l, h, first, n, g):
        part = pl.ds(first, n)
        return remote(
            rs_src.at[l, h, part, pl.ds(0, RSB[h])], rs_dst.at[l, h, part, pl.ds(0, RSB[h])],
            rs_send.at[l, h], rs_recv.at[l, h, g], partner,
        )

    def lx_copy(first, n):
        rows, k = pl.ds(first, n), int(first > 0)
        return remote(lx_src.at[rows], lx_dst.at[rows], lx_send.at[k], lx_recv.at[k], partner)

    def ex_copy(p, first, n):
        rows, k = pl.ds(first, n), int(first > 0)
        return remote(
            ex_src.at[rows], ex_dst.at[p, rows], ex_send.at[k], ex_recv.at[k], plane(p)
        )

    def ex_all(first, n):
        part, k = ex_dst.at[pl.ds(1, CHIPS - 1), pl.ds(first, n)], int(first > 0)
        return remote(part, part, ex_send.at[k], ex_recv.at[k], partner)

    def od_copy(d):
        return remote(
            od_src.at[(s + d) % 4], od_dst.at[s], od_send.at[d], od_recv.at[d], section(d)
        )

    def group_of(p, groups=GROUPS):
        return [g for g, (first, n) in enumerate(groups) if first <= p < first + n][0]

    barrier = pltpu.get_barrier_semaphore()
    peers = [plane(p) for p in reversed(range(1, CHIPS))]
    peers += [section(d) for d in (2, 1, 3)] + [partner]
    for peer in peers:
        pl.semaphore_signal(barrier, inc=1, device_id=peer, device_id_type=MESH)

    own_x = pltpu.make_async_copy(x_hbm.at[s], cur, loc_sem.at[0])
    own_x.start()
    own_a = pltpu.make_async_copy(
        a_hbm.at[0, :, :, pl.ds(pl.multiple_of(t * COLS, COLS), COLS)], a_own, loc_sem.at[1]
    )
    own_a.start()
    own_b = pltpu.make_async_copy(b_hbm.at[0], b_own, loc_sem.at[2])
    own_b.start()
    own_m = pltpu.make_async_copy(m_hbm.at[0], m_own, loc_sem.at[3])
    own_m.start()
    own_w = pltpu.make_async_copy(w_hbm.at[0], w_buf.at[s], loc_sem.at[4])
    own_w.start()
    own_g = pltpu.make_async_copy(g_hbm.at[s], grad, loc_sem.at[5])
    own_g.start()

    own_a.wait()
    own_b.wait()
    own_m.wait()
    for d in range(4):
        tenant = ten_ref[(s + d) % 4]
        pair = jnp.concatenate([a_own[tenant], b_own[tenant]], axis=0)
        mag = jnp.broadcast_to(m_own[pl.ds(tenant, 1), :], (8, COLS))
        if d == 0:
            sm_buf[s] = pair
            mg_buf[s] = mag
        else:
            sm_src[d] = pair
            mg_src[d] = mag
    own_x.wait()

    pl.semaphore_wait(barrier, len(peers))

    for d in (2, 1, 3):
        sm_copy(d).start()
        mg_copy(d).start()

    def send_block(l, h):
        xg[l, h, c, 0] = cur[h * H : (h + 1) * H]
        for p in reversed(range(1, CHIPS)):
            ag_copy(l, h, p, group_of(p)).start()
        cf_copy(l, h, 0, 1, 2, c).start()

    def split_stage(k):
        events = ROUTES[k][0]
        n = 0
        while n < len(events) and events[n][1] == k:
            n += 1
        return events[:n], events[n:]

    def send_events(k, events):
        for way, layer, first, n in events:

            def one(j):
                copy = w_copy(way, layer, first + j, layer == k)
                if layer != k:
                    copy.wait_recv()
                copy.start()

            every(n, one)

    def in_section(fn):
        for k in range(4):

            @pl.when(s == k)
            def _():
                fn(k)

    in_section(lambda k: send_events(k, split_stage(k)[0]))

    for h in range(NH):
        send_block(0, h)
    for d in range(1, 4):
        sm_copy(d).wait_recv()
        mg_copy(d).wait_recv()
    for l in range(L):
        ag_a[c, 0, l * R : (l + 1) * R] = sm_buf[l, 0:R]
    for p in reversed(range(1, CHIPS)):
        aa_copy(p, group_of(p)).start()

    in_section(lambda k: send_events(k, split_stage(k)[1]))
    own_w.wait()
    own_g.wait()

    for g, (first, n) in enumerate(GROUPS):
        aa_all(first, n, g).wait_recv()
    ac_copy(c).start()
    ac_copy(1 - c).wait_recv()

    def weights_of(k, l):
        if l:
            send_events(k, ROUTES[k].get(l, []))
        if l != k:
            for first, n in awaited(k, l, l):
                every(n, lambda j: w_copy(0, l, first + j, False).wait_recv())

    def a_rows(l, p):
        rows = pl.ds(pl.multiple_of(l * R, R), R)
        return jnp.concatenate([ag_a[0, p, rows, :], ag_a[1, p, rows, :]], axis=1)

    def local_grads(l):
        up = grad[...].astype(F32)
        gm = jnp.sum(up * sv_branch[l], axis=0, keepdims=True) / sv_norm[l, 0:1]
        res[l, R : 2 * R] = dot(sv_low[l], sv_gb[...], 0, 0)
        res[l, 2 * R : 2 * R + 8] = jnp.broadcast_to(gm, (8, COLS))

    def begin(l, h):
        tokens = slice(h * H, (h + 1) * H)
        branch = sv_branch[l, tokens]
        b_l = sm_buf[l, R : 2 * R]
        grad_branch = (grad[tokens].astype(F32) * sv_scale[l, 0:1]).astype(BF16)
        sv_gb[tokens] = grad_branch
        last = h == NH - 1
        if last:
            ce_src[l] = dot(b_l, sv_gb[...], 1, 1)
            ce_copy(l).start()
        rank = dot(grad_branch, b_l, 1, 1)
        rank_hi = rank.astype(BF16)
        rank_lo = (rank - rank_hi.astype(F32)).astype(BF16)
        rank_two = jnp.concatenate([rank_hi, rank_lo], axis=1)
        row = jnp.sum(grad_branch.astype(F32) * branch, axis=1, keepdims=True)
        share = row * (1.0 / D) / sv_root[l, tokens]

        def part(p):
            q = inverse(p)
            rows = w_buf[l, pl.ds(pl.multiple_of(source(q) * 256, 256), 256), :]
            a_q = a_rows(l, q)
            both = dot(grad_branch, rows, 1, 1) + dot(
                rank_two, jnp.concatenate([a_q, a_q], axis=0), 1, 0
            )
            zero = both[:, 0:COLS] - xg[l, h, 0, q].astype(F32) * share
            one = both[:, COLS:] - xg[l, h, 1, q].astype(F32) * share
            return jnp.where(c == 0, one, zero), jnp.where(c == 0, zero, one)

        def work(q):
            for p in range(RUNS[q], RUNS[q] + 8):
                theirs, mine = part(p)
                cs_src[l, h, p] = theirs.astype(BF16)
                mine_buf[p] = mine
            cs_copy(l, h, q).start()

        work(0)
        work(1)
        for q in range(2):
            if last and q == 0:
                ce_copy(l).wait_recv()
                ext = ce_src[l] + ce_dst[l]
                own_ext[...] = ext
                ext_b = ext.astype(BF16)
            cs_copy(l, h, q).wait_recv()
            for p in reversed(range(RUNS[q], RUNS[q] + 8)):
                total = mine_buf[p] + cs_dst[l, h, p].astype(F32)
                if p:
                    rs_src[l, h, p, 0:H] = total.astype(BF16)
                    if last:
                        rs_src[l, h, p, H : H + R] = ext_b
                    rs_copy(l, h, p, group_of(p, RS_GROUPS)).start()
                else:
                    own_sum[h] = total
        if last:
            local_grads(l)

    def normed_own(l):
        x_own = jnp.concatenate([xg[l, i, c, 0] for i in range(NH)], axis=0)
        return (x_own.astype(F32) / sv_root[l]).astype(BF16)

    def adapter_grad(l, rank_sum):
        res[l, 0:R] = fold3(dot(split3(rank_sum), normed_own(l), 1, 0))

    def finish(l, h):
        tokens = slice(h * H, (h + 1) * H)
        total = own_sum[h]
        rank_sum = own_ext[...]
        for g, (first, n) in enumerate(RS_GROUPS):
            rs_all(l, h, first, n, g).wait_recv()
            for p in range(first, first + n):
                total = total + rs_dst[l, h, p, 0:H].astype(F32)
                if h == NH - 1:
                    rank_sum = rank_sum + rs_dst[l, h, p, H : H + R].astype(F32)
        state = grad[tokens].astype(F32) + total / sv_root[l, tokens]
        grad[tokens] = state.astype(BF16)
        return rank_sum

    def w_rows(l, p):
        return w_buf[l, pl.ds(pl.multiple_of(source(p) * 256, 256), 256), :]

    def adapter_part(l):
        gram = jnp.zeros((R, R), F32)
        for p in range(CHIPS):
            a_p = a_rows(l, p)
            gram = gram + dot(a_p, a_p, 1, 1)
        return dot(gram, sm_buf[l, R : 2 * R].astype(F32), 1, 0, HIGHEST)

    def column_norms(l, quad):
        def squares(i, total):
            rows = w_buf[l, pl.ds(pl.multiple_of(i * 256, 256), 256), :].astype(F32)
            return total + jnp.sum((rows * rows).reshape(32, 8, COLS), axis=0)

        base_sq = jnp.sum(
            lax.fori_loop(0, 16, squares, jnp.zeros((8, COLS), F32)), axis=0, keepdims=True
        )
        cross = jnp.zeros((R, COLS), F32)
        for p in range(CHIPS):
            cross = cross + dot(a_rows(l, p), w_rows(l, p), 1, 0)
        b_wide = sm_buf[l, R : 2 * R].astype(F32)
        total = base_sq + jnp.sum(b_wide * (2.0 * cross + quad), axis=0, keepdims=True)
        norm = jnp.sqrt(total + 1e-06)
        sv_norm[l] = jnp.broadcast_to(norm, (8, COLS))
        sv_scale[l] = jnp.broadcast_to(mg_buf[l, 0:1] / norm, (8, COLS))

    def forward(l, _):
        quad = adapter_part(l)
        for layer in range(L):

            @pl.when(l == layer)
            def _():
                in_section(lambda k: weights_of(k, layer))

        column_norms(l, quad)
        for h in range(NH):
            tokens = slice(h * H, (h + 1) * H)
            acc = jnp.zeros((H, COLS), F32)
            low_acc = jnp.zeros((H, R), F32)
            ssq = jnp.zeros((H, COLS), F32)

            def use(first, n, g, acc, low_acc, ssq):
                cf_copy(l, h, first, n, g, 1 - c).wait_recv()
                for p in range(first, first + n):
                    both = jnp.concatenate([xg[l, h, 0, p], xg[l, h, 1, p]], axis=1)
                    acc = acc + dot(both, w_rows(l, p), 1, 0)
                    low_acc = low_acc + dot(both, a_rows(l, p), 1, 1)
                    wide = both.astype(F32)
                    wide = wide * wide
                    ssq = ssq + wide[:, 0:COLS] + wide[:, COLS:]
                return acc, low_acc, ssq

            before = (0, 1, 2)
            for g, (first, n) in enumerate(GROUPS):
                ag_all(l, h, first, n, g).wait_recv()
                cf_copy(l, h, first, n, g, c).start()
                acc, low_acc, ssq = use(*before, acc, low_acc, ssq)
                before = (first, n, g)
            acc, low_acc, ssq = use(*before, acc, low_acc, ssq)

            mean = jnp.sum(ssq, axis=1, keepdims=True) * (1.0 / D)
            root = jnp.sqrt(mean + 1e-05)
            inv = 1.0 / root
            low = (low_acc * inv).astype(BF16)
            branch = acc * inv + dot(low, sm_buf[l, R : 2 * R], 1, 0)
            sv_branch[l, tokens] = branch
            sv_low[l, tokens] = low
            sv_root[l, tokens] = jnp.broadcast_to(root, (H, COLS))
            state = cur[tokens].astype(F32) + sv_scale[l, 0:1] * branch
            cur[tokens] = state.astype(BF16)

            @pl.when(l < L - 1)
            def _():
                send_block(l + 1, h)

            @pl.when(l == L - 1)
            def _():
                begin(L - 1, h)

        return 0

    lax.fori_loop(0, L, forward, 0)

    def backward(i, _):
        l = L - 1 - i
        for h in range(NH):
            rank_sum = finish(l, h)
            if h == NH - 1:
                rank_buf[...] = rank_sum

            @pl.when(l > 1)
            def _():
                begin(l - 1, h)

        @pl.when(l > 1)
        def _():
            adapter_grad(l, rank_buf[...])

        return 0

    lax.fori_loop(0, L - 1, backward, 0)

    sv_gb[...] = (grad[...].astype(F32) * sv_scale[0, 0:1]).astype(BF16)
    lx_src[0:R] = dot(sm_buf[0, R : 2 * R], sv_gb[...], 1, 1)
    lx_copy(0, R).start()
    adapter_grad(1, rank_buf[...])
    local_grads(0)
    sum_a = jnp.zeros((1, COLS), F32)
    sum_b = jnp.zeros((1, COLS), F32)
    sum_m = jnp.zeros((1, COLS), F32)
    for l in range(L):
        if l:
            ga = res[l, 0:R]
            sum_a = sum_a + jnp.sum(ga * ga, axis=0, keepdims=True)
        gb = res[l, R : 2 * R]
        sum_b = sum_b + jnp.sum(gb * gb, axis=0, keepdims=True)
        gm = res[l, 2 * R : 2 * R + 1]
        sum_m = sum_m + gm * gm
    lx_src[R : R + 8] = jnp.concatenate([sum_a, sum_b, sum_m, jnp.zeros((5, COLS), F32)], axis=0)
    lx_copy(R, 8).start()
    lx_copy(0, R).wait_recv()
    rank_sum = lx_src[0:R] + lx_dst[0:R]
    ex_src[0:R] = rank_sum
    for p in reversed(range(1, CHIPS)):
        ex_copy(p, 0, R).start()
    lx_copy(R, 8).wait_recv()
    sums = lx_src[R : R + 8] + lx_dst[R : R + 8]
    ex_src[R : R + 8] = sums
    for p in reversed(range(1, CHIPS)):
        ex_copy(p, R, 8).start()
    normed = normed_own(0)
    outer = jnp.zeros((TOK, TOK), F32)
    for p in range(CHIPS):
        both = jnp.concatenate(
            [
                jnp.concatenate([xg[0, h, 0, p], xg[0, h, 1, p]], axis=1)
                for h in range(NH)
            ],
            axis=0,
        )
        outer = outer + dot(both, both, 1, 1)
    inv = 1.0 / sv_root[0]
    outer = outer * inv * inv.T
    outer_hi = outer.astype(BF16)
    outer_lo = (outer - outer_hi.astype(F32)).astype(BF16)
    right = jnp.concatenate([normed, outer_hi, outer_lo], axis=1)
    ex_all(R, 8).wait_recv()
    for p in range(1, CHIPS):
        sums = sums + ex_dst[p, R : R + 8]
    ex_all(0, R).wait_recv()
    for p in range(1, CHIPS):
        rank_sum = rank_sum + ex_dst[p, 0:R]
    made = fold3(dot(split3(rank_sum), right, 1, 0))
    res[0, 0:R] = made[:, 0:COLS]
    sq = rank_sum * (made[:, COLS : 2 * COLS] + made[:, 2 * COLS :])

    def norm_of(v, count):
        return 1.0 / jnp.sqrt(jnp.sum(v, axis=1, keepdims=True) * (1.0 / count) + 1e-06)

    by_a = norm_of(sums[0:1] + jnp.sum(sq, axis=0, keepdims=True), L * R * D)
    by_b = norm_of(sums[1:2], L * R * D)
    by_m = norm_of(sums[2:3], L * D)
    for l in range(L):
        od_src[l, 0:R] = res[l, 0:R] * by_a
        od_src[l, R : 2 * R] = res[l, R : 2 * R] * by_b
        od_src[l, 2 * R : 2 * R + 8] = res[l, 2 * R : 2 * R + 8] * by_m
    for d in (2, 1, 3):
        od_copy(d).start()
    od_dst[s] = od_src[s]

    def drain_w(k):
        for way in range(2):
            w_left(way, sent(k, way))

    in_section(drain_w)
    aa_all(1, CHIPS - 1, 0).wait_send()
    ac_copy(c).wait_send()

    def drain_l(l):
        for h in range(NH):
            ag_all(l, h, 1, CHIPS - 1, 0).wait_send()
            cf_copy(l, h, 0, 1, 2, c).wait_send()
            for g, (first, n) in enumerate(GROUPS):
                cf_copy(l, h, first, n, g, c).wait_send()

    every(L, drain_l)

    def drain_b(i):
        l = i + 1
        for h in range(NH):
            rs_all(l, h, 1, CHIPS - 1, 0).wait_send()
            for q in range(2):
                cs_copy(l, h, q).wait_send()
        ce_copy(l).wait_send()

    every(L - 1, drain_b)
    lx_copy(0, R).wait_send()
    lx_copy(R, 8).wait_send()
    ex_all(0, R).wait_send()
    ex_all(R, 8).wait_send()
    for d in range(1, 4):
        sm_copy(d).wait_send()
        mg_copy(d).wait_send()

    for d in (1, 3, 2):
        od_copy(d).wait_recv()
    for tenant in range(4):
        out = jnp.zeros((2 * R + 8, COLS), F32)
        for k in range(4):
            out = jnp.where(ten_ref[k] == tenant, od_dst[k], out)
        oa_ref[0, tenant] = out[0:R]
        ob_ref[0, tenant] = out[R : 2 * R]
        om_ref[0, pl.ds(tenant, 1), :] = out[2 * R : 2 * R + 1]
    for d in range(1, 4):
        od_copy(d).wait_send()


def local(inputs, grad_out, tenants, base_weight, adapter_a, adapter_b, magnitude):
    vmem = pl.BlockSpec(memory_space=pltpu.VMEM)
    hbm = pl.BlockSpec(memory_space=pl.ANY)
    dma = pltpu.SemaphoreType.DMA
    return pl.pallas_call(
        kernel,
        out_shape=(
            jax.ShapeDtypeStruct((1, 4, R, COLS), F32),
            jax.ShapeDtypeStruct((1, 4, R, COLS), F32),
            jax.ShapeDtypeStruct((1, 4, COLS), F32),
        ),
        in_specs=[pl.BlockSpec(memory_space=pltpu.SMEM)] + [hbm] * 6,
        out_specs=(vmem, vmem, vmem),
        scratch_shapes=[
            pltpu.VMEM((L, D, COLS), BF16),
            pltpu.VMEM((4, R, COLS), BF16),
            pltpu.VMEM((4, R, COLS), BF16),
            pltpu.VMEM((4, COLS), F32),
            pltpu.VMEM((4, 2 * R, COLS), BF16),
            pltpu.VMEM((4, 8, COLS), F32),
            pltpu.VMEM((4, 2 * R, COLS), BF16),
            pltpu.VMEM((4, 8, COLS), F32),
            pltpu.VMEM((2, CHIPS, L * R, COLS), BF16),
            pltpu.VMEM((L, NH, 2, CHIPS, H, COLS), BF16),
            pltpu.VMEM((TOK, COLS), BF16),
            pltpu.VMEM((TOK, COLS), BF16),
            pltpu.VMEM((L, TOK, COLS), F32),
            pltpu.VMEM((L, TOK, R), BF16),
            pltpu.VMEM((L, TOK, COLS), F32),
            pltpu.VMEM((L, 8, COLS), F32),
            pltpu.VMEM((L, 8, COLS), F32),
            pltpu.VMEM((TOK, COLS), BF16),
            pltpu.VMEM((CHIPS, H, COLS), F32),
            pltpu.VMEM((L, NH, CHIPS, H, COLS), BF16),
            pltpu.VMEM((L, NH, CHIPS, H, COLS), BF16),
            pltpu.VMEM((L, R, TOK), F32),
            pltpu.VMEM((L, R, TOK), F32),
            pltpu.VMEM((L, NH, CHIPS, H + R, COLS), BF16),
            pltpu.VMEM((L, NH, CHIPS, H + R, COLS), BF16),
            pltpu.VMEM((NH, H, COLS), F32),
            pltpu.VMEM((R, TOK), F32),
            pltpu.VMEM((R, TOK), F32),
            pltpu.VMEM((R + 8, TOK), F32),
            pltpu.VMEM((R + 8, TOK), F32),
            pltpu.VMEM((R + 8, TOK), F32),
            pltpu.VMEM((CHIPS, R + 8, TOK), F32),
            pltpu.VMEM((L, 2 * R + 8, COLS), F32),
            pltpu.VMEM((L, 2 * R + 8, COLS), F32),
            pltpu.VMEM((L, 2 * R + 8, COLS), F32),
            dma((6,)),
            dma((2,)),
            dma((L, WCH)),
            dma((4,)),
            dma((4,)),
            dma((4,)),
            dma((4,)),
            dma,
            dma((3,)),
            dma,
            dma,
            dma((L, NH)),
            dma((L, NH, 3)),
            dma((L, NH, 4)),
            dma((L, NH, 4)),
            dma((L, NH, 4)),
            dma((L, NH, 4)),
            dma((L,)),
            dma((L,)),
            dma((L, NH)),
            dma((L, NH, 3)),
            dma((2,)),
            dma((2,)),
            dma((2,)),
            dma((2,)),
            dma((4,)),
            dma((4,)),
        ],
        compiler_params=pltpu.CompilerParams(
            collective_id=0, has_side_effects=True, vmem_limit_bytes=60 * 2**20
        ),
    )(tenants, inputs, grad_out, base_weight, adapter_a, adapter_b, magnitude)


def solution(mesh):
    return jax.shard_map(
        local,
        mesh=mesh,
        in_specs=(
            P(None, None, "tensor"),
            P(None, None, "tensor"),
            P(),
            P("section", None, "tensor"),
            P("section", None, None, None),
            P("section", None, None, "tensor"),
            P("section", None, "tensor"),
        ),
        out_specs=(
            P("section", None, None, "tensor"),
            P("section", None, None, "tensor"),
            P("section", None, "tensor"),
        ),
        check_vma=False,
    )
```
